32 devices in a mesh: groups: 2 (over y), tensor: 4 (over z), pool: 2 (over x), inner: 2 (over core).
Axes of the slice: x: 2, y: 2, z: 4, core: 2. Of those that a mesh axis runs over, the one named last changes fastest.
Arguments:
- tokens: bfloat16 [3072, 8192], P(('groups', 'pool', 'inner'), 'tensor'), parts along dimension 0, may hold values from -6 to 6
- token_adapter_ids: int32 [3072], P(('groups', 'pool', 'inner')), parts along dimension 0, may hold values from 0 to 7, as said below
- adapter_pool_slot: int32 [16], P('groups'), parts along dimension 0, may hold values from 0 to 7, as said below
- adapter_rank_blocks: int32 [16], P('groups'), parts along dimension 0, may hold values from 1 to 8
- query_weight: bfloat16 [8192, 4096], P(None, 'tensor'), may hold values from -0.0625 to 0.0625
- pool_down_factors: bfloat16 [16, 128, 8192], P(('groups', 'pool', 'inner'), None, 'tensor'), parts along dimension 0, may hold values from -0.0625 to 0.0625
- pool_up_factors: bfloat16 [16, 128, 4096], P(('groups', 'pool', 'inner'), None, 'tensor'), parts along dimension 0, may hold values from -0.5 to 0.5
Outputs:
- query: bfloat16 [3072, 4096], P(('groups', 'pool', 'inner'), 'tensor'), parts along dimension 0
The draws below stay inside these ranges and needn't reach their ends.
There are 2 independent parts, one for each index of `groups`. The reference program is written for one: setup_inputs(seed, part) draws one part's arguments, and reference() takes and returns one part's arrays. A program takes and returns all parts, laid end to end along the dimension named above; an argument that names none is the same for every part. Nothing has to cross between parts.
Inputs may be any that keep to these rules, and one draw needn't show every extreme that they name: `token_adapter_ids`: of the 384 tokens of one device (aligned blocks of the token order), at most 192 have adapters whose slots lie in one aligned group of 2 slots (slots g * 2 to (g + 1) * 2 - 1); in every draw one such group receives exactly 192 tokens from every device. `adapter_pool_slot`: A permutation of the adapters over the slots.
All inputs are finite; a program needn't handle non-finite values.
Results may differ from the reference program's by a relative error of at most 0.0046.
Values may be sent and summed in bfloat16 or wider, within the bound.
No kernel may reach another device: no remote copies, remote signals or barrier semaphores. Data moves between devices by JAX's collectives and lax.ppermute only.
A program may use at most 128 MiB of HBM per device.

```python
import jax
import jax.numpy as jnp
from jax import lax

MODEL_WIDTH = 8192
MAXIMUM_RANK = 128
RBLK = 16
TOK_DEV = 384
ADP_DEV = 2
QUERY_COLUMNS = 4096
OWNERS = 4
CAP = 192
ADAPTER_COUNT = 8
TOKENS = 1536


def share_layout(key):
    order = jax.random.permutation(jax.random.fold_in(key, 11), ADAPTER_COUNT).astype(jnp.int32)
    hottest = jax.random.randint(jax.random.fold_in(key, 12), (), 0, OWNERS).astype(jnp.int32)
    place = jnp.arange(TOK_DEV, dtype=jnp.int32)
    others = max(OWNERS - 1, 1)
    offset = jnp.where(place < CAP, 0, 1 + (place - CAP) % others).astype(jnp.int32)
    homes = (hottest + offset) % OWNERS
    shuffle_keys = jax.random.split(jax.random.fold_in(key, 13), OWNERS)
    orders = jax.vmap(lambda k: jax.random.permutation(k, TOK_DEV))(shuffle_keys)
    owners = homes[orders].astype(jnp.int32)
    local = jax.random.randint(jax.random.fold_in(key, 14), (OWNERS, TOK_DEV), 0, ADP_DEV).astype(jnp.int32)
    adapters = order[owners * ADP_DEV + local].reshape(-1).astype(jnp.int32)
    return (order, adapters)


def draw_token_adapter_ids(key, part):
    order, adapters = share_layout(key)
    return adapters


def draw_adapter_pool_slot(key, part):
    order, adapters = share_layout(key)
    return jnp.argsort(order, stable=True).astype(jnp.int32)


def plant(drawn, own_key, smallest, top_value):
    index_at = [jax.random.randint(jax.random.fold_in(own_key, axis), (), 0, length) for axis, length in enumerate(drawn.shape)]
    longest = drawn.shape.index(max(drawn.shape))
    next_to = index_at[:longest] + [(index_at[longest] + 1) % drawn.shape[longest]] + index_at[longest + 1:]
    return drawn.at[tuple(index_at)].set(smallest).at[tuple(next_to)].set(top_value)


def block_levels(rng, dims, pieces, smallest, largest):
    gain, own = 1.0, jax.random.fold_in(rng, 6)
    for dim, parts in pieces:
        steps = jnp.exp(jax.random.uniform(jax.random.fold_in(own, dim), (parts,), jnp.float32, smallest / len(pieces), largest / len(pieces)))
        gain = gain * jnp.repeat(steps, dims[dim] // parts).reshape([-1 if axis == dim else 1 for axis in range(len(dims))])
    return gain


def normal_values(rng, extent, spread, reach, cuts=(), held_as=jnp.bfloat16):
    values = spread * jax.random.normal(rng, extent, jnp.float32)
    if cuts:
        values = values * block_levels(rng, extent, cuts, -0.22, 0.18)
    return jnp.clip(values, -reach, reach).astype(held_as)


def setup_inputs(seed: int = 0, part: int = 0) -> dict:
    splits = jax.random.split(jax.random.key(seed), 8)
    part_splits = jax.random.split(jax.random.fold_in(splits[7], part), 8)
    return {
        "tokens": normal_values(part_splits[0], (TOKENS, MODEL_WIDTH), 1.0, 6.0, ((0, 4), (1, 4))),
        "token_adapter_ids": draw_token_adapter_ids(jax.random.fold_in(jax.random.fold_in(splits[7], part), 71), part),
        "adapter_pool_slot": draw_adapter_pool_slot(jax.random.fold_in(jax.random.fold_in(splits[7], part), 71), part),
        "adapter_rank_blocks": plant(jax.random.randint(part_splits[3], (ADAPTER_COUNT,), 1, MAXIMUM_RANK // RBLK + 1), jax.random.fold_in(part_splits[3], 1), 1, (MAXIMUM_RANK // RBLK + 1) - 1).astype(jnp.int32),
        "query_weight": normal_values(splits[4], (MODEL_WIDTH, QUERY_COLUMNS), MODEL_WIDTH ** -0.5, 0.0625, ((1, 4),)),
        "pool_down_factors": normal_values(part_splits[5], (ADAPTER_COUNT, MAXIMUM_RANK, MODEL_WIDTH), MODEL_WIDTH ** -0.5, 0.0625, ((0, 4), (2, 4))),
        "pool_up_factors": normal_values(part_splits[6], (ADAPTER_COUNT, MAXIMUM_RANK, QUERY_COLUMNS), MAXIMUM_RANK ** -0.5, 0.5, ((0, 4), (2, 4))),
    }


def reference(tokens, token_adapter_ids, adapter_pool_slot, adapter_rank_blocks, query_weight, pool_down_factors, pool_up_factors):
    slot = jnp.take(adapter_pool_slot, token_adapter_ids).astype(jnp.int32)
    rank = (RBLK * jnp.take(adapter_rank_blocks, token_adapter_ids)).astype(jnp.int32)
    base = jnp.dot(tokens, query_weight, preferred_element_type=jnp.float32)
    keep = jnp.arange(MAXIMUM_RANK, dtype=jnp.int32)[None, :] < rank[:, None]

    def down_factor(total, item):
        index, factor = item
        part = lax.dot_general(tokens, factor, (((1,), (1,)), ((), ())), preferred_element_type=jnp.float32)
        chosen = jnp.logical_and((slot == index)[:, None], keep)
        return total + jnp.where(chosen, part, 0.0), None

    block_start = jnp.zeros((tokens.shape[0], MAXIMUM_RANK), jnp.float32)
    rank_activations, unused_value = lax.scan(down_factor, block_start, (jnp.arange(ADAPTER_COUNT, dtype=jnp.int32), pool_down_factors))
    rank_activations = rank_activations.astype(jnp.bfloat16)

    def up_factor(total, item):
        index, factor = item
        part = jnp.dot(rank_activations, factor, preferred_element_type=jnp.float32)
        return total + jnp.where((slot == index)[:, None], part, 0.0), None

    zero_update = jnp.zeros((tokens.shape[0], query_weight.shape[1]), jnp.float32)
    query_update, unused_value = lax.scan(up_factor, zero_update, (jnp.arange(ADAPTER_COUNT, dtype=jnp.int32), pool_up_factors))
    query_update = query_update.astype(jnp.bfloat16)
    return (base + query_update.astype(jnp.float32)).astype(jnp.bfloat16)
```

```python
import functools

import jax
import jax.numpy as jnp
from jax import lax
from jax.experimental import pallas as pl
from jax.experimental.pallas import tpu as pltpu
from jax.sharding import PartitionSpec as P

MAXIMUM_RANK = 128
RBLK = 16
AXES = ("groups", "tensor", "pool", "inner")

PAIRS = [(0, 1), (1, 0), (2, 3), (3, 2)]
MIDDLE = [(1, 2), (2, 1)]
OUTWARD = [(1, 0), (2, 3)]
INWARD = [(0, 1), (3, 2)]
STEPS = 4


def lookup(indices, table):
    count = table.shape[0]
    match = indices[..., None] == jnp.arange(count, dtype=jnp.int32)
    return jnp.sum(jnp.where(match, table, 0), axis=-1)


def swap(x, axis):
    return lax.ppermute(x, axis, [(0, 1), (1, 0)])


def hop(x, pairs):
    return lax.ppermute(x, "tensor", pairs)


def after(x, *others):
    return lax.optimization_barrier((x,) + others)[0]


def owner_mask(owner, slot, rank, adapters):
    local = slot - owner * adapters
    which = local[:, None, None] == jnp.arange(adapters, dtype=jnp.int32)[None, :, None]
    within = jnp.arange(MAXIMUM_RANK, dtype=jnp.int32)[None, None, :] < rank[:, None, None]
    return jnp.logical_and(which, within)


def project_down(tokens, down, mask):
    flat = down.reshape(-1, down.shape[2])
    coords = lax.dot_general(
        tokens, flat, (((1,), (1,)), ((), ())), preferred_element_type=jnp.float32
    )
    return jnp.sum(jnp.where(mask, coords.reshape(mask.shape), 0.0), axis=1)


def project_up(coords, up, mask):
    spread = jnp.where(mask, coords[:, None, :], jnp.zeros((), jnp.bfloat16))
    spread = spread.reshape(coords.shape[0], -1)
    flat = up.reshape(-1, up.shape[2])
    return jnp.dot(spread, flat, preferred_element_type=jnp.float32)


def add_dot(out_ref, a, b):
    out_ref[...] += jnp.dot(a, b, preferred_element_type=jnp.float32)


def cost(rows, depth, columns):
    return pl.CostEstimate(
        flops=2 * rows * depth * columns,
        bytes_accessed=2 * (rows * depth + depth * columns) + 4 * rows * columns,
        transcendentals=0,
    )


def own_block(tokens, weight, index, depth=512):
    rows, width = tokens.shape
    columns = weight.shape[1]
    steps = width // depth

    def body(index_ref, a_ref, w_ref, out_ref):
        @pl.when(pl.program_id(0) == 0)
        def _():
            out_ref[...] = jnp.zeros_like(out_ref)

        add_dot(out_ref, a_ref[...], w_ref[...])

    return pl.pallas_call(
        body,
        out_shape=jax.ShapeDtypeStruct((rows, columns), jnp.float32),
        grid_spec=pltpu.PrefetchScalarGridSpec(
            num_scalar_prefetch=1,
            grid=(steps,),
            in_specs=[
                pl.BlockSpec((rows, depth), lambda k, i: (0, k)),
                pl.BlockSpec((depth, columns), lambda k, i: (i[0] * steps + k, 0)),
            ],
            out_specs=pl.BlockSpec((rows, columns), lambda k, i: (0, 0)),
        ),
        cost_estimate=cost(rows, width, columns),
        compiler_params=pltpu.CompilerParams(vmem_limit_bytes=24 << 20),
    )(index.reshape(1).astype(jnp.int32), tokens, weight)


def near_blocks(total, outer, inner, across, relayed, weight, end, partner, near, depth=512):
    rows, width = outer.shape
    columns = weight.shape[1]
    steps = width // depth
    half = relayed.shape[1] // depth
    count = len(inner)
    size = rows // count

    def body(s_ref, *refs):
        inner_refs = refs[:count]
        outer_ref, across_ref, relayed_ref, w_ref, total_ref, out_ref = refs[count:]
        k = pl.program_id(0)
        at_end = s_ref[0] == 1

        @pl.when(k == 0)
        def _():
            out_ref[...] = total_ref[...]

        @pl.when(jnp.logical_and(k < steps, at_end))
        def _():
            add_dot(out_ref, outer_ref[...], w_ref[...])

        @pl.when(jnp.logical_and(k < steps, jnp.logical_not(at_end)))
        def _():
            a = jnp.concatenate([r[...] for r in inner_refs], axis=0)
            add_dot(out_ref, a, w_ref[...])

        @pl.when(jnp.logical_and(jnp.logical_and(k >= steps, k < steps + half), at_end))
        def _():
            add_dot(out_ref, relayed_ref[...], w_ref[...])

        @pl.when(jnp.logical_and(k >= steps, jnp.logical_not(at_end)))
        def _():
            add_dot(out_ref, across_ref[...], w_ref[...])

    first = lambda k, s: (0, jnp.minimum(k, steps - 1))
    second = lambda k, s: (0, jnp.maximum(k - steps, 0))
    some = lambda k, s: (0, jnp.clip(k - steps, 0, half - 1))
    rows_of = lambda k, s: (
        jnp.where(k < steps, s[1] * steps + k, s[2] * steps + k - steps),
        0,
    )
    whole = lambda k, s: (0, 0)
    scalars = jnp.stack([end.astype(jnp.int32), partner, near]).astype(jnp.int32)
    return pl.pallas_call(
        body,
        out_shape=jax.ShapeDtypeStruct((rows, columns), jnp.float32),
        grid_spec=pltpu.PrefetchScalarGridSpec(
            num_scalar_prefetch=1,
            grid=(2 * steps,),
            in_specs=[pl.BlockSpec((size, depth), first)] * count
            + [
                pl.BlockSpec((rows, depth), first),
                pl.BlockSpec((rows, depth), second),
                pl.BlockSpec((rows, depth), some),
                pl.BlockSpec((depth, columns), rows_of),
                pl.BlockSpec((rows, columns), whole),
            ],
            out_specs=pl.BlockSpec((rows, columns), whole),
        ),
        cost_estimate=cost(rows, 2 * width, columns),
        compiler_params=pltpu.CompilerParams(vmem_limit_bytes=32 << 20),
    )(scalars, *inner, outer, across, relayed, weight, total)


def far_block(total, far, weight, index, place, depth=512):
    size, width = far[0].shape
    rows = size * len(far)
    columns = weight.shape[1]
    steps = width // depth

    def body(index_ref, *refs):
        *far_refs, w_ref, total_ref, out_ref = refs

        @pl.when(pl.program_id(0) == 0)
        def _():
            out_ref[...] = total_ref[...]

        a = jnp.concatenate([r[...] for r in far_refs], axis=0)
        add_dot(out_ref, a, w_ref[...])

    return pl.pallas_call(
        body,
        out_shape=jax.ShapeDtypeStruct((rows, columns), jnp.float32),
        grid_spec=pltpu.PrefetchScalarGridSpec(
            num_scalar_prefetch=1,
            grid=(steps,),
            in_specs=[pl.BlockSpec((size, depth), lambda k, i: (0, k))] * len(far)
            + [
                pl.BlockSpec((depth, columns), lambda k, i: (i[0] * steps + k, 0)),
                pl.BlockSpec((rows, columns), lambda k, i: (place, 0)),
            ],
            out_specs=pl.BlockSpec((rows, columns), lambda k, i: (0, 0)),
        ),
        cost_estimate=cost(rows, width, columns),
        compiler_params=pltpu.CompilerParams(vmem_limit_bytes=24 << 20),
    )(index.reshape(1).astype(jnp.int32), *far, weight, total)


def helped(far, across, place, pieces):
    size, width = far[0].shape
    rows = size * len(far)
    columns = pieces[0][1].shape[1]
    deep = width // len(pieces)
    half = width // 2
    shallow = half // len(pieces)

    def body(place_ref, *refs):
        far_refs = refs[: len(far)]
        across_ref = refs[len(far)]
        piece_refs = refs[len(far) + 1 : -1]
        out_ref = refs[-1]
        total = jnp.zeros(out_ref.shape, jnp.float32)
        for i, piece_ref in enumerate(piece_refs):
            q = place_ref[i]
            columns_far = pl.ds(pl.multiple_of(q * deep, deep), deep)
            columns_near = pl.ds(pl.multiple_of(q * shallow, shallow), shallow)
            a = jnp.concatenate([r[:, columns_far] for r in far_refs], axis=0)
            total += jnp.dot(a, piece_ref[:deep, :], preferred_element_type=jnp.float32)
            total += jnp.dot(
                across_ref[:, columns_near],
                piece_ref[deep:, :],
                preferred_element_type=jnp.float32,
            )
        out_ref[...] = total.astype(out_ref.dtype)

    whole = lambda k, s: (0, 0)
    return pl.pallas_call(
        body,
        out_shape=jax.ShapeDtypeStruct((rows, columns), jnp.bfloat16),
        grid_spec=pltpu.PrefetchScalarGridSpec(
            num_scalar_prefetch=1,
            grid=(1,),
            in_specs=[pl.BlockSpec((size, width), whole)] * len(far)
            + [pl.BlockSpec((rows, half), lambda k, s: (place, 1))]
            + [pl.BlockSpec(pieces[0][1].shape, whole)] * len(pieces),
            out_specs=pl.BlockSpec((rows, columns), whole),
        ),
        cost_estimate=cost(rows, width + half, columns),
        compiler_params=pltpu.CompilerParams(vmem_limit_bytes=40 << 20),
    )(
        jnp.stack([q for q, _ in pieces]).astype(jnp.int32),
        *far,
        across,
        *[piece for _, piece in pieces],
    )


def chained(tokens, slot, rank, weight, down, up):
    rows, width = tokens.shape
    adapters = down.shape[0]
    size = rows // STEPS
    z = lax.axis_index("tensor")
    end = jnp.logical_or(z == 0, z == 3)
    mine = lax.axis_index(("pool", "inner"))
    seat = lax.axis_index(("groups", "pool", "inner"))
    partner, near, far = z ^ 1, jnp.where(end, 3 - (z ^ 1), 3 - z), 3 - (z ^ 1)
    deep, shallow = width // 8, width // 16

    def part(i):
        return tokens[i * size : (i + 1) * size]

    piece = jnp.concatenate(
        [
            lax.dynamic_slice_in_dim(weight, (3 - z) * width + seat * deep, deep, 0),
            lax.dynamic_slice_in_dim(
                weight, near * width + width // 2 + seat * shallow, shallow, 0
            ),
        ],
        axis=0,
    )
    across = hop(tokens, MIDDLE)
    lent = hop(piece, INWARD)
    outer = hop(tokens, OUTWARD)
    down_x = swap(down, "pool")
    inner = [hop(part(0), INWARD), hop(part(1), INWARD), hop(part(2), INWARD)]
    down_c, up_c = swap(down, "inner"), swap(up, "inner")
    total = own_block(tokens, weight, z)
    masks = [owner_mask(mine ^ r, slot, rank, adapters) for r in range(4)]
    coords = project_down(tokens, down, masks[0]) + project_down(tokens, down_c, masks[1])

    lent_y, lent_x = swap(lent, "groups"), swap(lent, "pool")
    lent_c = swap(lent, "inner")
    up_x = swap(after(up, lent), "pool")
    down_xc = swap(down_x, "inner")
    coords = coords + project_down(tokens, down_x, masks[2])
    coords = coords + project_down(tokens, down_xc, masks[3])
    coords = coords.astype(jnp.bfloat16)
    pair = coords.astype(jnp.float32) + hop(coords, PAIRS).astype(jnp.float32)
    pair = pair.astype(jnp.bfloat16)
    inner.append(hop(after(part(3), coords), INWARD))
    relayed = hop(across[:, : width // 2], OUTWARD)
    beyond = [hop(inner[0], MIDDLE), hop(inner[1], MIDDLE)]
    lent_d = swap(lent_x, "groups")
    lent_yc, lent_xc = swap(lent_y, "inner"), swap(lent_x, "inner")
    whole = (pair.astype(jnp.float32) + hop(pair, MIDDLE).astype(jnp.float32)).astype(
        jnp.bfloat16
    )
    beyond.append(hop(after(inner[2], pair), MIDDLE))
    beyond.append(hop(inner[3], MIDDLE))
    low_rank = jnp.where(end, hop(whole, OUTWARD), whole)
    up_xc = swap(up_x, "inner")
    lent_dc = swap(lent_d, "inner")
    pieces = [
        (seat, lent),
        (seat ^ 1, lent_c),
        (seat ^ 2, lent_x),
        (seat ^ 3, lent_xc),
        (seat ^ 4, lent_y),
        (seat ^ 5, lent_yc),
        (seat ^ 6, lent_d),
        (seat ^ 7, lent_dc),
    ]
    total = near_blocks(total, outer, inner, across, relayed, weight, end, partner, near)
    delta = 0.0
    for mask, factors in zip(masks, (up, up_c, up_x, up_xc)):
        delta = delta + project_up(low_rank, factors, mask)
    total = total + delta.astype(jnp.bfloat16).astype(jnp.float32)
    early = hop(helped(beyond[:3], across, 0, pieces), OUTWARD)
    total_early = far_block(total, beyond[:3], weight, far, 0)
    late = hop(helped(beyond[3:], across, 3, pieces), OUTWARD)
    total_late = far_block(total, beyond[3:], weight, far, 3)
    return (
        jnp.concatenate([total_early, total_late], axis=0)
        + jnp.concatenate([early, late], axis=0).astype(jnp.float32)
    ).astype(jnp.bfloat16)


def gathered(tokens, slot, rank, weight, down, up):
    axes = ("pool", "inner")
    adapters = down.shape[0]
    base = jnp.dot(
        lax.all_gather(tokens, "tensor", axis=1, tiled=True),
        weight,
        preferred_element_type=jnp.float32,
    )
    downs = lax.all_gather(down, axes, axis=0, tiled=True)
    ups = lax.all_gather(up, axes, axis=0, tiled=True)
    mask = owner_mask(0, slot, rank, adapters * lax.axis_size(axes))
    coords = lax.psum(project_down(tokens, downs, mask), "tensor").astype(jnp.bfloat16)
    delta = project_up(coords, ups, mask).astype(jnp.bfloat16)
    return (base + delta.astype(jnp.float32)).astype(jnp.bfloat16)


def shards(
    tokens,
    token_adapter_ids,
    adapter_pool_slot,
    adapter_rank_blocks,
    query_weight,
    pool_down_factors,
    pool_up_factors,
):
    slot = lookup(token_adapter_ids, adapter_pool_slot)
    rank = RBLK * lookup(token_adapter_ids, adapter_rank_blocks)
    whole_chain = tuple(lax.axis_size(a) for a in AXES) == (2, 4, 2, 2)
    run = chained if whole_chain else gathered
    return run(tokens, slot, rank, query_weight, pool_down_factors, pool_up_factors)


def solution(mesh):
    in_specs = (
        P(("groups", "pool", "inner"), "tensor"),
        P(("groups", "pool", "inner")),
        P("groups"),
        P("groups"),
        P(None, "tensor"),
        P(("groups", "pool", "inner"), None, "tensor"),
        P(("groups", "pool", "inner"), None, "tensor"),
    )
    out_specs = P(("groups", "pool", "inner"), "tensor")
    return jax.shard_map(shards, mesh=mesh, in_specs=in_specs, out_specs=out_specs, check_vma=False)
```

```python
import jax
import jax.numpy as jnp
from jax import lax
from jax.experimental import pallas as pl
from jax.experimental.pallas import tpu as pltpu
from jax.sharding import PartitionSpec as P

MAXIMUM_RANK = 128
RBLK = 16
AXES = ("groups", "tensor", "pool", "inner")

PAIRS = [(0, 1), (1, 0), (2, 3), (3, 2)]
MIDDLE = [(1, 2), (2, 1)]
OUTWARD = [(1, 0), (2, 3)]
INWARD = [(0, 1), (3, 2)]


def lookup(indices, table):
    count = table.shape[0]
    match = indices[..., None] == jnp.arange(count, dtype=jnp.int32)
    return jnp.sum(jnp.where(match, table, 0), axis=-1)


def slot_and_rank(ids, slots, blocks):
    return lookup(ids, slots), RBLK * lookup(ids, blocks)


def swap(x, axis):
    return lax.ppermute(x, axis, [(0, 1), (1, 0)])


def hop(x, pairs):
    return lax.ppermute(x, "tensor", pairs)


VMEM = pl.BlockSpec(memory_space=pltpu.VMEM)
ANY = pl.BlockSpec(memory_space=pl.ANY)
HBM = pl.BlockSpec(memory_space=pltpu.HBM)


def call(held, body, out_shapes, operands, in_specs, out_specs=None, scratch=(), room=16):
    single = not isinstance(out_shapes, list)
    shapes = [out_shapes] if single else out_shapes
    out_specs = out_specs or [VMEM] * len(shapes)
    ins, outs = len(operands), len(shapes)
    tick = held["tick"]

    def counted(*refs):
        into = refs[ins + 1 + outs]
        into[...] = refs[ins][...] + 1.0
        body(*refs[:ins], *refs[ins + 1 : ins + 1 + outs], *refs[ins + 2 + outs :])

    *results, held["tick"] = pl.pallas_call(
        counted,
        out_shape=[*shapes, jax.ShapeDtypeStruct(tick.shape, tick.dtype)],
        in_specs=[*in_specs, VMEM],
        out_specs=[*out_specs, VMEM],
        scratch_shapes=list(scratch),
        cost_estimate=pl.CostEstimate(flops=10**12, bytes_accessed=0, transcendentals=0),
        compiler_params=pltpu.CompilerParams(vmem_limit_bytes=room << 20),
    )(*operands, tick)
    return results[0] if single else results


def fence(held):
    call(held, lambda: None, [], [], [])
    names = sorted(held)
    held.update(zip(names, lax.optimization_barrier(tuple(held[n] for n in names))))


def array(*shape, dtype=jnp.bfloat16):
    return jax.ShapeDtypeStruct(shape, dtype)


def dot(a, b):
    return jnp.dot(a, b, preferred_element_type=jnp.float32)


class Place:
    def __init__(self):
        z = lax.axis_index("tensor")
        self.own, self.partner = z, z ^ 1
        self.end = jnp.logical_or(z == 0, z == 3)
        self.near = jnp.where(self.end, 3 - self.partner, 3 - z)
        self.far = jnp.where(self.end, 3 - z, 3 - self.partner)
        self.seat = lax.axis_index(("groups", "pool", "inner"))
        self.mine = lax.axis_index(("pool", "inner"))


class Layout:
    def __init__(self, tokens, weight):
        self.tall, self.width = tokens.shape
        self.columns = weight.shape[1]
        self.deep, self.shallow = self.width // 8, self.width // 32
        self.lent = 8 * self.shallow
        self.rows = (self.deep + self.shallow) // 2
        self.spans = [
            (0, 0, 0, self.rows),
            (self.rows, 0, 1, self.deep - self.rows),
            (0, self.deep - self.rows, 1, self.shallow),
        ]
        self.cut = self.tall * 7 // 12
        self.sizes = [self.cut, self.tall - self.cut]

    def parts(self, ref):
        for first, at, side, size in self.spans:
            columns = pl.ds(side * self.columns, self.columns)
            yield first, size, ref.at[pl.ds(at, size), columns]


def run_copies(copies):
    for copy in copies:
        copy.start()
    for copy in copies:
        copy.wait()


def first_rows(held, tokens, weight, layout):
    width, rows = layout.width, layout.rows

    def body(t_ref, w_ref, out_ref, sem):
        place = Place()

        @pl.when(place.end)
        def _():
            far = place.far * width + place.seat * layout.deep
            near = (place.near + 1) * width - (8 - place.seat) * layout.shallow
            lend = []
            for i, (first, size, into) in enumerate(layout.parts(out_ref)):
                at = pl.multiple_of((far if i < 2 else near) + first, 32)
                lend.append(
                    pltpu.make_async_copy(w_ref.at[pl.ds(at, size)], into, sem.at[i])
                )
            run_copies(lend)

        @pl.when(jnp.logical_not(place.end))
        def _():
            run_copies(
                [pltpu.make_async_copy(t_ref.at[pl.ds(0, rows)], out_ref, sem.at[0])]
            )

    return call(
        held,
        body,
        array(rows, width),
        [tokens, weight],
        [HBM, HBM],
        scratch=[pltpu.SemaphoreType.DMA((3,))],
    )


def cut_up(held, tokens, layout):
    tall, width, rows, cut = layout.tall, layout.width, layout.rows, layout.cut
    cuts = [(rows, tall - rows), (0, cut), (cut, tall - cut)]

    def body(t_ref, *refs):
        *into_refs, all_ref, sem = refs
        run_copies([pltpu.make_async_copy(t_ref, all_ref, sem.at[0])])
        run_copies(
            [
                pltpu.make_async_copy(all_ref.at[pl.ds(at, size)], into, sem.at[i])
                for i, ((at, size), into) in enumerate(zip(cuts, into_refs))
            ]
        )

    return call(
        held,
        body,
        [array(size, width) for _, size in cuts],
        [tokens],
        [ANY],
        [ANY] * len(cuts),
        [pltpu.VMEM((tall, width), tokens.dtype), pltpu.SemaphoreType.DMA((3,))],
    )


def left_columns(held, x, layout):
    keep = layout.width - layout.lent

    def body(x_ref, out_ref, sem):
        run_copies([pltpu.make_async_copy(x_ref.at[:, pl.ds(0, keep)], out_ref, sem)])

    shape = array(x.shape[0], keep)
    return call(held, body, shape, [x], [ANY], [VMEM], [pltpu.SemaphoreType.DMA])


class Rows:
    def __init__(self, x_ref, start, depth):
        self.x_ref, self.start, self.depth = x_ref, start, depth

    def dot(self, a_ref, limit=None):
        some = pl.ds(pl.multiple_of(self.start, 128), limit or self.depth)
        return dot(a_ref[...] if limit is None else a_ref[:, :limit], self.x_ref[some, :])


def started(*copies):
    for copy in copies:
        copy.start()
    return copies


def waited(copies):
    for copy in copies:
        copy.wait()


def sums(layout):
    return array(layout.tall, layout.columns, dtype=jnp.float32)


def sums_room(layout):
    return [
        pltpu.VMEM((layout.tall, layout.columns), jnp.float32),
        pltpu.SemaphoreType.DMA((8,)),
    ]


def own_block(held, tokens, weight, layout):
    def body(a_ref, w_ref, out_ref, a_held, sum_ref, sem):
        load = started(pltpu.make_async_copy(a_ref, a_held, sem.at[0]))
        w = Rows(w_ref, Place().own * layout.width, layout.width)
        waited(load)
        sum_ref[...] = w.dot(a_held)
        run_copies([pltpu.make_async_copy(sum_ref, out_ref, sem.at[1])])

    return call(
        held,
        body,
        sums(layout),
        [tokens, weight],
        [ANY, VMEM],
        [HBM],
        [pltpu.VMEM((layout.tall, layout.width), jnp.bfloat16)] + sums_room(layout),
    )


def add_partner(held, total, first, rest, inner, beyond, weight, layout):
    width, tall, cut, rows = layout.width, layout.tall, layout.cut, layout.rows

    def body(total_ref, first_ref, rest_ref, in0_ref, in1_ref, beyond_ref, w_ref, *refs):
        out_ref, p_held, f_held, sum_ref, sem = refs
        place = Place()

        def into(x_ref, at, size, i):
            return pltpu.make_async_copy(x_ref, p_held.at[pl.ds(at, size)], sem.at[i])

        at_end = [into(first_ref, 0, rows, 0), into(rest_ref, rows, tall - rows, 1)]
        inside = [
            into(in0_ref, 0, cut, 0),
            into(in1_ref, cut, tall - cut, 1),
            pltpu.make_async_copy(beyond_ref, f_held, sem.at[2]),
        ]

        @pl.when(place.end)
        def _():
            started(*at_end)

        @pl.when(jnp.logical_not(place.end))
        def _():
            started(*inside)

        more = started(pltpu.make_async_copy(total_ref, sum_ref, sem.at[3]))
        p = Rows(w_ref, place.partner * width, width)
        f = Rows(w_ref, place.far * width, width)

        @pl.when(place.end)
        def _():
            waited(at_end)
            waited(more)
            sum_ref[...] += p.dot(p_held)

        @pl.when(jnp.logical_not(place.end))
        def _():
            waited(inside)
            waited(more)
            sum_ref[...] += p.dot(p_held)
            sum_ref[:cut, :] += f.dot(f_held)

        run_copies([pltpu.make_async_copy(sum_ref, out_ref, sem.at[4])])

    return call(
        held,
        body,
        sums(layout),
        [total, first, rest, *inner, beyond, weight],
        [ANY] * 6 + [VMEM],
        [HBM],
        [pltpu.VMEM((size, width), jnp.bfloat16) for size in (tall, cut)]
        + sums_room(layout),
    )


def add_last(held, total, low, use, ups, relayed, across, beyond, term, weight, layout):
    adapters, rank, columns = ups[0].shape
    count = len(ups)
    cut, last = layout.sizes
    tall, width = layout.tall, layout.width
    keep = width - layout.lent

    def body(hop_ref, low_ref, use_ref, *refs):
        up_refs = refs[:count]
        total_ref, relayed_ref, across_ref, b_ref, term_ref, w_ref = refs[count : count + 6]
        out_ref, late_ref, n_held, b_held, t_held, first_ref, sum_ref, sem = refs[count + 6 :]
        place = Place()
        at_end = [pltpu.make_async_copy(relayed_ref, n_held.at[:, pl.ds(0, keep)], sem.at[0])]
        inside = [
            pltpu.make_async_copy(across_ref, n_held, sem.at[0]),
            pltpu.make_async_copy(b_ref, b_held, sem.at[1]),
        ]

        @pl.when(place.end)
        def _():
            started(*at_end)

        @pl.when(jnp.logical_not(place.end))
        def _():
            started(*inside)

        more = started(
            pltpu.make_async_copy(total_ref, sum_ref, sem.at[2]),
            pltpu.make_async_copy(term_ref, t_held, sem.at[3]),
        )
        n = Rows(w_ref, place.near * width, width)
        f = Rows(w_ref, place.far * width, width)
        low = jnp.where(place.end, hop_ref[...], low_ref[...])
        terms = 0.0
        for turn, up_ref in enumerate(up_refs):
            owner = place.mine ^ turn
            some = [
                jnp.where(use_ref[...] == owner * adapters + j, low, 0)
                for j in range(adapters)
            ]
            terms += dot(jnp.concatenate(some, axis=1), up_ref[...])
        waited(more)
        sum_ref[...] += terms.astype(jnp.bfloat16).astype(jnp.float32)
        sum_ref[:cut, :] += t_held[...].astype(jnp.float32)

        @pl.when(place.end)
        def _():
            waited(at_end)
            sum_ref[...] += n.dot(n_held, keep)

        @pl.when(jnp.logical_not(place.end))
        def _():
            waited(inside)
            sum_ref[...] += n.dot(n_held)
            sum_ref[cut:, :] += f.dot(b_held)

        first_ref[...] = sum_ref[:cut, :].astype(first_ref.dtype)
        run_copies(
            [
                pltpu.make_async_copy(first_ref, out_ref.at[pl.ds(0, cut)], sem.at[4]),
                pltpu.make_async_copy(sum_ref.at[pl.ds(cut, last)], late_ref, sem.at[5]),
            ]
        )

    return call(
        held,
        body,
        [array(tall, columns), array(last, columns, dtype=jnp.float32)],
        [*low, use, *[u.reshape(-1, columns) for u in ups]]
        + [total, relayed, across, beyond, term, weight],
        [VMEM] * (3 + count) + [ANY] * 5 + [VMEM],
        [ANY, ANY],
        [
            pltpu.VMEM((tall, width), jnp.bfloat16),
            pltpu.VMEM((last, width), jnp.bfloat16),
            pltpu.VMEM((cut, columns), jnp.bfloat16),
            pltpu.VMEM((cut, columns), jnp.bfloat16),
        ]
        + sums_room(layout),
    )


def helped(held, beyond, across, pieces, layout, i):
    half, width, columns = layout.sizes[i], layout.width, layout.columns
    start = i * layout.cut
    count = len(pieces)
    deep, shallow, lent = layout.deep, layout.shallow, layout.lent

    def body(beyond_ref, across_ref, *refs):
        piece_refs = refs[:count]
        out_ref, b_held, a_held, deep_ref, near_ref, sem = refs[count:]
        seat = Place().seat
        copies = started(
            pltpu.make_async_copy(beyond_ref, b_held, sem.at[0]),
            pltpu.make_async_copy(
                across_ref.at[pl.ds(start, half), pl.ds(width - lent, lent)],
                a_held,
                sem.at[1],
            ),
        )
        lends = []
        for k, piece_ref in enumerate(piece_refs):
            for j, (first, size, part) in enumerate(layout.parts(piece_ref)):
                if j < 2:
                    into = deep_ref.at[pl.ds(k * deep + first, size)]
                else:
                    at = pl.multiple_of((seat ^ k) * shallow, shallow)
                    into = near_ref.at[pl.ds(at, size)]
                lends.append(pltpu.make_async_copy(part, into, sem.at[2 + 3 * k + j]))
        started(*lends)
        waited(copies)
        total = 0.0
        step = count // 2
        for first in (0, step):
            turns = range(first, first + step)
            blocks = [
                b_held[:, pl.ds(pl.multiple_of((seat ^ k) * deep, deep), deep)] for k in turns
            ]
            waited(lends[3 * first : 3 * (first + step)])
            some = deep_ref[first * deep : (first + step) * deep, :]
            total += dot(jnp.concatenate(blocks, axis=1), some)
        total += dot(a_held[...], near_ref[...])
        out_ref[...] = total.astype(out_ref.dtype)

    return call(
        held,
        body,
        array(half, columns),
        [beyond, across, *pieces],
        [ANY] * (2 + count),
        scratch=[
            pltpu.VMEM((half, width), jnp.bfloat16),
            pltpu.VMEM((half, lent), jnp.bfloat16),
            pltpu.VMEM((deep * count, columns), jnp.bfloat16),
            pltpu.VMEM((lent, columns), jnp.bfloat16),
            pltpu.SemaphoreType.DMA((2 + 3 * count,)),
        ],
    )


def finished(held, out, late, term, layout):
    kept = [held[n] for n in sorted(held) if n != "tick"]
    cut, last = layout.sizes

    def body(out_ref, late_ref, term_ref, *refs):
        into_ref, sum_ref, sem = refs[len(kept) :]
        sum_ref[...] = (late_ref[...] + term_ref[...].astype(jnp.float32)).astype(
            sum_ref.dtype
        )
        run_copies([pltpu.make_async_copy(sum_ref, into_ref.at[pl.ds(cut, last)], sem)])

    return pl.pallas_call(
        body,
        out_shape=array(*out.shape),
        in_specs=[ANY, VMEM, VMEM] + [ANY] * len(kept),
        out_specs=ANY,
        scratch_shapes=[
            pltpu.VMEM((last, layout.columns), out.dtype),
            pltpu.SemaphoreType.DMA,
        ],
        input_output_aliases={0: 0},
        compiler_params=pltpu.CompilerParams(vmem_limit_bytes=16 << 20),
    )(out, late, term, *kept)


def coords_of(held, tokens, use, downs, turns, before=None):
    adapters, rank = downs[0].shape[0], downs[0].shape[1]
    count = len(downs)

    def body(use_ref, tokens_ref, *refs):
        out_ref, sent_ref = refs[-2:]
        mine = Place().mine
        total = refs[count][...] if before is not None else 0.0
        for turn, down_ref in zip(turns, refs[:count]):
            coords = lax.dot_general(
                tokens_ref[...],
                down_ref[...],
                (((1,), (1,)), ((), ())),
                preferred_element_type=jnp.float32,
            )
            for j in range(adapters):
                some = coords[:, j * rank : (j + 1) * rank]
                mask = use_ref[...] == (mine ^ turn) * adapters + j
                total = total + jnp.where(mask, some, 0.0)
        out_ref[...] = total
        sent_ref[...] = total.astype(sent_ref.dtype)

    flat = [d.reshape(-1, d.shape[2]) for d in downs]
    more = [] if before is None else [before]
    shape = (tokens.shape[0], rank)
    return call(
        held,
        body,
        [array(*shape, dtype=jnp.float32), array(*shape)],
        [use, tokens, *flat, *more],
        [VMEM] * (2 + count + len(more)),
    )


def added(held, a, b):
    def body(a_ref, b_ref, out_ref):
        sums = a_ref[...].astype(jnp.float32) + b_ref[...].astype(jnp.float32)
        out_ref[...] = sums.astype(out_ref.dtype)

    return call(held, body, array(*a.shape), [a, b], [VMEM] * 2)


def chained(tokens, tables, weight, down, up):
    layout = Layout(tokens, weight)
    across = hop(tokens, MIDDLE)
    h = dict(tick=jnp.zeros((8, 128), jnp.float32), down=down, up=up, tokens=tokens)
    h["ids"], h["slots"], h["blocks"] = tables
    fence(h)
    down_x, down_c = swap(h["down"], "pool"), swap(h["down"], "inner")
    h["first"] = first_rows(h, h["tokens"], weight, layout)
    fence(h)
    first_p = hop(h["first"], PAIRS)
    h["rest"], h["part0"], h["part1"] = cut_up(h, h["tokens"], layout)
    slot, rank = slot_and_rank(h.pop("ids"), h.pop("slots"), h.pop("blocks"))
    row = jnp.arange(MAXIMUM_RANK, dtype=jnp.int32)[None, :]
    h["use"] = jnp.where(row < rank[:, None], slot[:, None], -1)
    h["down_c"] = down_c
    fence(h)
    inner0 = hop(h["part0"], INWARD)
    fence(h)
    rest_o = hop(h["rest"], OUTWARD)
    total = own_block(h, h["tokens"], weight, layout)
    h["lent"] = first_p
    fence(h)
    lent_y = swap(h["lent"], "groups")
    h["down_x"] = down_x
    fence(h)
    lent_x = swap(h["lent"], "pool")
    downs = [h["down"], h["down_c"], h["down_x"]]
    coords, _ = coords_of(h, h["tokens"], h["use"], downs, [0, 1, 2])
    h["across"] = across
    fence(h)
    inner1 = hop(h["part1"], INWARD)
    h["left"] = left_columns(h, h["across"], layout)
    h["lent_y"], h["inner0"] = lent_y, inner0
    fence(h)
    beyond0 = hop(h["inner0"], MIDDLE)
    h["rest_o"], h["lent_x"] = rest_o, lent_x
    fence(h)
    lent_d = swap(h["lent_x"], "groups")
    fence(h)
    relayed = hop(h["left"], OUTWARD)
    fence(h)
    down_xc = swap(h["down_x"], "inner")
    h["down_xc"] = down_xc
    fence(h)
    lent_c = swap(h["lent"], "inner")
    coords, h["coords"] = coords_of(h, h["tokens"], h["use"], [h["down_xc"]], [3], coords)
    h["lent_c"] = lent_c
    fence(h)
    coords_p = hop(h["coords"], INWARD)
    h["inner1"] = inner1
    fence(h)
    lent_yc = swap(h["lent_y"], "inner")
    h["coords_p"], h["lent_yc"] = coords_p, lent_yc
    fence(h)
    h["pair"] = added(h, coords, h["coords_p"])
    fence(h)
    pair_m = hop(h["pair"], MIDDLE)
    h["beyond0"] = beyond0
    fence(h)
    beyond1 = hop(h["inner1"], MIDDLE)
    h["pair_m"], h["lent_d"] = pair_m, lent_d
    fence(h)
    lent_xc, lent_dc = swap(h["lent_x"], "inner"), swap(h["lent_d"], "inner")
    h["whole"] = added(h, h["pair"], h["pair_m"])
    h["lent_xc"], h["lent_dc"] = lent_xc, lent_dc
    fence(h)
    low_o = hop(h["whole"], OUTWARD)
    up_x = swap(h["up"], "pool")
    fence(h)
    names = ("lent", "lent_c", "lent_x", "lent_xc", "lent_y", "lent_yc", "lent_d", "lent_dc")
    pieces = [h[n] for n in names]
    h["help0"] = helped(h, h["beyond0"], h["across"], pieces, layout, 0)
    fence(h)
    help_o0 = hop(h["help0"], OUTWARD)
    fence(h)
    total = add_partner(
        h,
        total,
        h["lent"],
        h["rest_o"],
        [h["inner0"], h["inner1"]],
        h["beyond0"],
        weight,
        layout,
    )
    h["beyond1"] = beyond1
    h["relayed"], h["up_x"], h["low_o"] = relayed, up_x, low_o
    fence(h)
    up_xc, up_c = swap(h["up_x"], "inner"), swap(h["up"], "inner")
    pieces = [h[n] for n in names]
    h["help1"] = helped(h, h["beyond1"], h["across"], pieces, layout, 1)
    h["up_xc"], h["up_c"] = up_xc, up_c
    fence(h)
    help_o1 = hop(h["help1"], OUTWARD)
    h["help_o0"] = help_o0
    fence(h)
    out, late = add_last(
        h,
        total,
        [h["low_o"], h["whole"]],
        h["use"],
        [h["up"], h["up_c"], h["up_x"], h["up_xc"]],
        h["relayed"],
        h["across"],
        h["beyond1"],
        h["help_o0"],
        weight,
        layout,
    )
    h["help_o1"] = help_o1
    fence(h)
    return finished(h, out, late, h.pop("help_o1"), layout)


def owner_mask(slot, rank, adapters):
    which = slot[:, None, None] == jnp.arange(adapters, dtype=jnp.int32)[None, :, None]
    within = jnp.arange(MAXIMUM_RANK, dtype=jnp.int32)[None, None, :] < rank[:, None, None]
    return jnp.logical_and(which, within)


def gathered(tokens, tables, weight, down, up):
    slot, rank = slot_and_rank(*tables)
    axes = ("pool", "inner")
    base = jnp.dot(
        lax.all_gather(tokens, "tensor", axis=1, tiled=True),
        weight,
        preferred_element_type=jnp.float32,
    )
    downs = lax.all_gather(down, axes, axis=0, tiled=True)
    ups = lax.all_gather(up, axes, axis=0, tiled=True)
    mask = owner_mask(slot, rank, downs.shape[0])
    coords = lax.dot_general(
        tokens,
        downs.reshape(-1, downs.shape[2]),
        (((1,), (1,)), ((), ())),
        preferred_element_type=jnp.float32,
    ).reshape(mask.shape)
    coords = jnp.sum(jnp.where(mask, coords, 0.0), axis=1)
    low_rank = lax.psum(coords, "tensor").astype(jnp.bfloat16)
    spread = jnp.where(mask, low_rank[:, None, :], jnp.zeros((), jnp.bfloat16))
    delta = jnp.dot(
        spread.reshape(spread.shape[0], -1),
        ups.reshape(-1, ups.shape[2]),
        preferred_element_type=jnp.float32,
    ).astype(jnp.bfloat16)
    return (base + delta.astype(jnp.float32)).astype(jnp.bfloat16)


def shards(
    tokens,
    token_adapter_ids,
    adapter_pool_slot,
    adapter_rank_blocks,
    query_weight,
    pool_down_factors,
    pool_up_factors,
):
    tables = (token_adapter_ids, adapter_pool_slot, adapter_rank_blocks)
    whole_chain = tuple(lax.axis_size(a) for a in AXES) == (2, 4, 2, 2)
    run = chained if whole_chain else gathered
    return run(tokens, tables, query_weight, pool_down_factors, pool_up_factors)


def solution(mesh):
    in_specs = (
        P(("groups", "pool", "inner"), "tensor"),
        P(("groups", "pool", "inner")),
        P("groups"),
        P("groups"),
        P(None, "tensor"),
        P(("groups", "pool", "inner"), None, "tensor"),
        P(("groups", "pool", "inner"), None, "tensor"),
    )
    out_specs = P(("groups", "pool", "inner"), "tensor")
    return jax.shard_map(shards, mesh=mesh, in_specs=in_specs, out_specs=out_specs, check_vma=False)
```

```python
import itertools

import jax
import jax.numpy as jnp
import numpy as np
from jax import lax
from jax.experimental import pallas as pl
from jax.experimental.pallas import tpu as pltpu
from jax.sharding import PartitionSpec as P

MAXIMUM_RANK = 128
RBLK = 16
AXES = ("groups", "tensor", "pool", "inner")

PAIRS = [(0, 1), (1, 0), (2, 3), (3, 2)]
OUTWARD = [(1, 0), (2, 3)]
INWARD = [(0, 1), (3, 2)]


def lookup(indices, table):
    count = table.shape[0]
    match = indices[..., None] == jnp.arange(count, dtype=jnp.int32)
    return jnp.sum(jnp.where(match, table, 0), axis=-1)


def slot_and_rank(ids, slots, blocks):
    return lookup(ids, slots), RBLK * lookup(ids, blocks)


def swap(x, axis):
    return lax.ppermute(x, axis, [(0, 1), (1, 0)])


def inside(x, step):
    shape = (2, 4, 2, 2)
    pairs = []
    for place in itertools.product(*map(range, shape)):
        groups, z, pool, inner = place
        to = step(*place) if z in (1, 2) else (groups, z, pool, 1 - inner)
        pairs.append(tuple(int(np.ravel_multi_index(p, shape)) for p in (place, to)))
    return lax.ppermute(x, AXES, pairs)


def hop_middle(x):
    return inside(x, lambda g, z, p, i: (g, 3 - z, p, i))


def swap_inside(x, axis):
    steps = {
        "groups": lambda g, z, p, i: (1 - g, z, p, i),
        "pool": lambda g, z, p, i: (g, z, 1 - p, i),
        "inner": lambda g, z, p, i: (g, z, p, 1 - i),
    }
    return inside(x, steps[axis])


def hop(x, pairs):
    return lax.ppermute(x, "tensor", pairs)


VMEM = pl.BlockSpec(memory_space=pltpu.VMEM)
ANY = pl.BlockSpec(memory_space=pl.ANY)
HBM = pl.BlockSpec(memory_space=pltpu.HBM)


def call(held, body, out_shapes, operands, in_specs, out_specs=None, scratch=(), room=16, alias=None):
    single = not isinstance(out_shapes, list)
    shapes = [out_shapes] if single else out_shapes
    out_specs = out_specs or [VMEM] * len(shapes)
    ins, outs = len(operands), len(shapes)
    tick = held["tick"]

    def counted(*refs):
        into = refs[ins + 1 + outs]
        into[...] = refs[ins][...] + 1.0
        body(*refs[:ins], *refs[ins + 1 : ins + 1 + outs], *refs[ins + 2 + outs :])

    *results, held["tick"] = pl.pallas_call(
        counted,
        out_shape=[*shapes, jax.ShapeDtypeStruct(tick.shape, tick.dtype)],
        in_specs=[*in_specs, VMEM],
        out_specs=[*out_specs, VMEM],
        scratch_shapes=list(scratch),
        input_output_aliases=alias or {},
        cost_estimate=pl.CostEstimate(flops=10**12, bytes_accessed=0, transcendentals=0),
        compiler_params=pltpu.CompilerParams(vmem_limit_bytes=room << 20),
    )(*operands, tick)
    return results[0] if single else results


def fence(held):
    call(held, lambda: None, [], [], [])
    names = sorted(held)
    held.update(zip(names, lax.optimization_barrier(tuple(held[n] for n in names))))


def array(*shape, dtype=jnp.bfloat16):
    return jax.ShapeDtypeStruct(shape, dtype)


def dot(a, b):
    return jnp.dot(a, b, preferred_element_type=jnp.float32)


class Place:
    def __init__(self):
        z = lax.axis_index("tensor")
        self.own, self.partner = z, z ^ 1
        self.end = jnp.logical_or(z == 0, z == 3)
        self.near = jnp.where(self.end, 3 - self.partner, 3 - z)
        self.far = jnp.where(self.end, 3 - z, 3 - self.partner)
        self.seat = lax.axis_index(("groups", "pool", "inner"))
        self.mine = lax.axis_index(("pool", "inner"))


class Layout:
    def __init__(self, tokens, weight):
        self.tall, self.width = tokens.shape
        self.columns = weight.shape[1]
        self.deep = self.width // 8
        self.rows = self.deep // 2
        self.cut = self.tall * 7 // 12
        self.sizes = [self.cut, self.tall - self.cut]

    def sides(self, ref):
        for side in range(2):
            columns = pl.ds(side * self.columns, self.columns)
            yield side * self.rows, ref.at[:, columns]


def run_copies(copies):
    for copy in copies:
        copy.start()
    for copy in copies:
        copy.wait()


LARGE = 50


def first_rows(held, tokens, weight, layout):
    rows = layout.rows

    def body(t_ref, w_ref, out_ref, sem):
        place = Place()

        @pl.when(place.end)
        def _():
            start = place.far * layout.width + place.seat * layout.deep
            run_copies(
                [
                    pltpu.make_async_copy(
                        w_ref.at[pl.ds(pl.multiple_of(start + first, rows), rows)],
                        into,
                        sem.at[i],
                    )
                    for i, (first, into) in enumerate(layout.sides(out_ref))
                ]
            )

        @pl.when(jnp.logical_not(place.end))
        def _():
            run_copies(
                [pltpu.make_async_copy(t_ref.at[pl.ds(0, rows)], out_ref, sem.at[0])]
            )

    return call(
        held,
        body,
        array(rows, layout.width),
        [tokens, weight],
        [HBM, HBM],
        scratch=[pltpu.SemaphoreType.DMA((2,))],
        room=LARGE,
    )


def cut_up(held, tokens, layout):
    tall, width, rows, cut = layout.tall, layout.width, layout.rows, layout.cut
    cuts = [(rows, tall - rows), (0, cut), (cut, tall - cut)]

    def body(t_ref, *refs):
        *into_refs, all_ref, sem = refs
        run_copies([pltpu.make_async_copy(t_ref, all_ref, sem.at[0])])
        run_copies(
            [
                pltpu.make_async_copy(all_ref.at[pl.ds(at, size)], into, sem.at[i])
                for i, ((at, size), into) in enumerate(zip(cuts, into_refs))
            ]
        )

    return call(
        held,
        body,
        [array(size, width) for _, size in cuts],
        [tokens],
        [ANY],
        [ANY] * len(cuts),
        [pltpu.VMEM((tall, width), tokens.dtype), pltpu.SemaphoreType.DMA((3,))],
    )


PARTS = 4


class Rows:
    def __init__(self, x_ref, start, held_ref, sem):
        self.depth, self.held_ref, self.copies = held_ref.shape[0] // PARTS, held_ref, []
        for i in range(PARTS):
            some = pl.ds(pl.multiple_of(start + i * self.depth, 128), self.depth)
            self.copies.append(
                pltpu.make_async_copy(
                    x_ref.at[some], held_ref.at[pl.ds(i * self.depth, self.depth)], sem.at[i]
                )
            )
        for copy in self.copies:
            copy.start()

    def dot(self, a_ref):
        total = 0.0
        for i, copy in enumerate(self.copies):
            copy.wait()
            some = pl.ds(i * self.depth, self.depth)
            total += dot(a_ref[:, some], self.held_ref[some, :])
        return total


def started(*copies):
    for copy in copies:
        copy.start()
    return copies


def waited(copies):
    for copy in copies:
        copy.wait()


def room(count, layout):
    shape = (layout.width, layout.columns)
    return [
        x
        for _ in range(count)
        for x in (pltpu.VMEM(shape, jnp.bfloat16), pltpu.SemaphoreType.DMA((PARTS,)))
    ]


def sums(layout):
    return array(layout.tall, layout.columns, dtype=jnp.float32)


def sums_room(layout):
    return [
        pltpu.VMEM((layout.tall, layout.columns), jnp.float32),
        pltpu.SemaphoreType.DMA((9,)),
    ]


def own_block(held, tokens, weight, layout):
    def body(a_ref, w_ref, out_ref, held_ref, w_sem, a_held, sum_ref, sem):
        load = started(pltpu.make_async_copy(a_ref, a_held, sem.at[0]))
        w = Rows(w_ref, Place().own * layout.width, held_ref, w_sem)
        waited(load)
        sum_ref[...] = w.dot(a_held)
        run_copies([pltpu.make_async_copy(sum_ref, out_ref, sem.at[1])])

    return call(
        held,
        body,
        sums(layout),
        [tokens, weight],
        [ANY, HBM],
        [HBM],
        room(1, layout)
        + [pltpu.VMEM((layout.tall, layout.width), jnp.bfloat16)]
        + sums_room(layout),
        room=LARGE,
    )


def add_block(held, total, at_end, inside, weight, layout):
    width, tall = layout.width, layout.tall
    arrays = [x for side in (at_end, inside) if side for x in side[1]]

    def body(total_ref, w_ref, *refs):
        array_refs = list(refs[: len(arrays)])
        out_ref, w_held, w_sem, a_held, sum_ref, sem = refs[len(arrays) :]
        place = Place()

        def run(name, part_refs):
            w = Rows(w_ref, getattr(place, name) * width, w_held, w_sem)
            loads, start = [], 0
            for i, ref in enumerate(part_refs):
                into = a_held.at[pl.ds(start, ref.shape[0])]
                loads.append(pltpu.make_async_copy(ref, into, sem.at[i]))
                start += ref.shape[0]
            started(*loads)
            more = started(pltpu.make_async_copy(total_ref, sum_ref, sem.at[3]))
            waited(loads)
            some = w.dot(a_held)
            waited(more)
            sum_ref[...] += some
            run_copies([pltpu.make_async_copy(sum_ref, out_ref, sem.at[4])])

        for side, here in ((at_end, place.end), (inside, jnp.logical_not(place.end))):
            if side:
                mine = [array_refs.pop(0) for _ in side[1]]
                pl.when(here)(lambda side=side, mine=mine: run(side[0], mine))

    return call(
        held,
        body,
        sums(layout),
        [total, weight, *arrays],
        [ANY, HBM] + [ANY] * len(arrays),
        [ANY],
        room(1, layout) + [pltpu.VMEM((tall, width), jnp.bfloat16)] + sums_room(layout),
        room=LARGE,
        alias={0: 0},
    )


def add_last(held, total, low, use, ups, relayed, beyond, term, weight, layout):
    adapters, rank, columns = ups[0].shape
    count = len(ups)
    cut, last = layout.sizes
    tall, width = layout.tall, layout.width

    def body(hop_ref, low_ref, use_ref, *refs):
        up_refs = refs[:count]
        total_ref, relayed_ref, b0_ref, b1_ref, term_ref, w_ref = refs[count : count + 6]
        out_ref, late_ref, *scratch = refs[count + 6 :]
        w_held, w_sem, a_held, t_held, u_held, first_ref, sum_ref, sem = scratch
        place = Place()
        at_end = [pltpu.make_async_copy(relayed_ref, a_held, sem.at[0])]
        inside = [
            pltpu.make_async_copy(b0_ref, a_held.at[pl.ds(0, cut)], sem.at[0]),
            pltpu.make_async_copy(b1_ref, a_held.at[pl.ds(cut, last)], sem.at[1]),
        ]

        loads = started(
            *[
                pltpu.make_async_copy(
                    up_ref,
                    u_held.at[pl.ds(i * adapters * rank, adapters * rank)],
                    sem.at[i + 3],
                )
                for i, up_ref in enumerate(up_refs)
            ],
            pltpu.make_async_copy(total_ref, sum_ref, sem.at[2]),
        )

        @pl.when(place.end)
        def _():
            started(*at_end)

        @pl.when(jnp.logical_not(place.end))
        def _():
            started(*inside)

        w = Rows(w_ref, jnp.where(place.end, place.near, place.far) * width, w_held, w_sem)
        more = started(pltpu.make_async_copy(term_ref, t_held, sem.at[7]))
        low = jnp.where(place.end, hop_ref[...], low_ref[...])
        some = [
            jnp.where(use_ref[...] == (place.mine ^ turn) * adapters + j, low, 0)
            for turn in range(count)
            for j in range(adapters)
        ]
        spread = jnp.concatenate(some, axis=1)
        waited(loads)
        terms = dot(spread, u_held[...])
        sum_ref[...] += terms.astype(jnp.bfloat16).astype(jnp.float32)

        @pl.when(place.end)
        def _():
            waited(at_end)

        @pl.when(jnp.logical_not(place.end))
        def _():
            waited(inside)

        sum_ref[...] += w.dot(a_held)
        waited(more)
        late = started(
            pltpu.make_async_copy(sum_ref.at[pl.ds(cut, last)], late_ref, sem.at[0])
        )
        first_ref[...] = (sum_ref[:cut, :] + t_held[...].astype(jnp.float32)).astype(
            first_ref.dtype
        )
        run_copies([pltpu.make_async_copy(first_ref, out_ref.at[pl.ds(0, cut)], sem.at[1])])
        waited(late)

    return call(
        held,
        body,
        [array(tall, columns), array(last, columns, dtype=jnp.float32)],
        [*low, use, *[u.reshape(-1, columns) for u in ups]]
        + [total, relayed, *beyond, term, weight],
        [VMEM] * 3 + [ANY] * (count + 5) + [HBM],
        [ANY, ANY],
        room(1, layout)
        + [
            pltpu.VMEM((tall, width), jnp.bfloat16),
            pltpu.VMEM((cut, columns), jnp.bfloat16),
            pltpu.VMEM((count * adapters * rank, columns), jnp.bfloat16),
            pltpu.VMEM((cut, columns), jnp.bfloat16),
        ]
        + sums_room(layout),
        room=LARGE,
    )


def helped(held, beyond, pieces, layout, i):
    size, width, columns = layout.sizes[i], layout.width, layout.columns
    count, deep = len(pieces), layout.deep

    def body(beyond_ref, *refs):
        piece_refs = refs[:count]
        out_ref, b_held, w_held, sem = refs[count:]
        seat = Place().seat
        load = started(pltpu.make_async_copy(beyond_ref, b_held, sem.at[0]))
        lends = started(
            *[
                pltpu.make_async_copy(
                    part,
                    w_held.at[pl.ds(k * deep + first, layout.rows)],
                    sem.at[1 + 2 * k + side],
                )
                for k, piece_ref in enumerate(piece_refs)
                for side, (first, part) in enumerate(layout.sides(piece_ref))
            ]
        )
        waited(load)
        total = 0.0
        step = count // 4
        for first in range(0, count, step):
            blocks = [
                b_held[:, pl.ds(pl.multiple_of((seat ^ k) * deep, deep), deep)]
                for k in range(first, first + step)
            ]
            waited(lends[2 * first : 2 * (first + step)])
            some = w_held[first * deep : (first + step) * deep, :]
            total += dot(jnp.concatenate(blocks, axis=1), some)
        out_ref[...] = total.astype(out_ref.dtype)

    return call(
        held,
        body,
        array(size, columns),
        [beyond, *pieces],
        [ANY] * (1 + count),
        scratch=[
            pltpu.VMEM((size, width), jnp.bfloat16),
            pltpu.VMEM((width, columns), jnp.bfloat16),
            pltpu.SemaphoreType.DMA((1 + 2 * count,)),
        ],
    )


def finished(held, out, late, term, layout):
    kept = [held[n] for n in sorted(held) if n != "tick"]
    cut, last = layout.sizes

    def body(out_ref, late_ref, term_ref, *refs):
        into_ref, sum_ref, sem = refs[len(kept) :]
        sum_ref[...] = (late_ref[...] + term_ref[...].astype(jnp.float32)).astype(
            sum_ref.dtype
        )
        run_copies([pltpu.make_async_copy(sum_ref, into_ref.at[pl.ds(cut, last)], sem)])

    return pl.pallas_call(
        body,
        out_shape=array(*out.shape),
        in_specs=[ANY, VMEM, VMEM] + [ANY] * len(kept),
        out_specs=ANY,
        scratch_shapes=[
            pltpu.VMEM((last, layout.columns), out.dtype),
            pltpu.SemaphoreType.DMA,
        ],
        input_output_aliases={0: 0},
        compiler_params=pltpu.CompilerParams(vmem_limit_bytes=16 << 20),
    )(out, late, term, *kept)


def coords_of(held, tokens, use, downs, turns, before=None):
    adapters, rank = downs[0].shape[0], downs[0].shape[1]
    count = len(downs)

    def body(use_ref, tokens_ref, *refs):
        out_ref, sent_ref = refs[-2:]
        mine = Place().mine
        total = refs[count][...] if before is not None else 0.0
        for turn, down_ref in zip(turns, refs[:count]):
            coords = lax.dot_general(
                tokens_ref[...],
                down_ref[...],
                (((1,), (1,)), ((), ())),
                preferred_element_type=jnp.float32,
            )
            for j in range(adapters):
                some = coords[:, j * rank : (j + 1) * rank]
                mask = use_ref[...] == (mine ^ turn) * adapters + j
                total = total + jnp.where(mask, some, 0.0)
        out_ref[...] = total
        sent_ref[...] = total.astype(sent_ref.dtype)

    flat = [d.reshape(-1, d.shape[2]) for d in downs]
    more = [] if before is None else [before]
    shape = (tokens.shape[0], rank)
    return call(
        held,
        body,
        [array(*shape, dtype=jnp.float32), array(*shape)],
        [use, tokens, *flat, *more],
        [VMEM] * (2 + count + len(more)),
    )


def added(held, a, b):
    def body(a_ref, b_ref, out_ref):
        sums = a_ref[...].astype(jnp.float32) + b_ref[...].astype(jnp.float32)
        out_ref[...] = sums.astype(out_ref.dtype)

    return call(held, body, array(*a.shape), [a, b], [VMEM] * 2)


def chained(tokens, tables, weight, down, up):
    layout = Layout(tokens, weight)
    across = hop_middle(tokens)
    h = dict(tick=jnp.zeros((8, 128), jnp.float32), down=down, up=up, tokens=tokens)
    h["ids"], h["slots"], h["blocks"] = tables
    fence(h)
    down_x, down_c = swap(h["down"], "pool"), swap(h["down"], "inner")
    h["first"] = first_rows(h, h["tokens"], weight, layout)
    fence(h)
    first_p = hop(h["first"], PAIRS)
    h["rest"], h["part0"], h["part1"] = cut_up(h, h["tokens"], layout)
    slot, rank = slot_and_rank(h.pop("ids"), h.pop("slots"), h.pop("blocks"))
    row = jnp.arange(MAXIMUM_RANK, dtype=jnp.int32)[None, :]
    h["use"] = jnp.where(row < rank[:, None], slot[:, None], -1)
    h["down_c"] = down_c
    fence(h)
    inner0 = hop(h["part0"], INWARD)
    fence(h)
    rest_o = hop(h["rest"], OUTWARD)
    total = own_block(h, h["tokens"], weight, layout)
    h["lent"] = first_p
    fence(h)
    lent_y = swap_inside(h["lent"], "groups")
    h["down_x"] = down_x
    fence(h)
    down_xc = swap(h["down_x"], "inner")
    downs = [h["down"], h["down_c"], h["down_x"]]
    coords, _ = coords_of(h, h["tokens"], h["use"], downs, [0, 1, 2])
    h["down_xc"] = down_xc
    fence(h)
    lent_x = swap_inside(h["lent"], "pool")
    fence(h)
    coords, h["coords"] = coords_of(h, h["tokens"], h["use"], [h["down_xc"]], [3], coords)
    h["lent_y"] = lent_y
    fence(h)
    coords_p = hop(h["coords"], INWARD)
    h["across"] = across
    fence(h)
    relayed = hop(h["across"], OUTWARD)
    h["inner0"] = inner0
    fence(h)
    beyond0 = hop_middle(h["inner0"])
    h["rest_o"], h["coords_p"] = rest_o, coords_p
    fence(h)
    inner1 = hop(h["part1"], INWARD)
    h["lent_x"] = lent_x
    fence(h)
    lent_d = swap_inside(h["lent_x"], "groups")
    fence(h)
    h["pair"] = added(h, coords, h["coords_p"])
    fence(h)
    pair_m = hop_middle(h["pair"])
    fence(h)
    at_end = ("partner", [h["lent"], h["rest_o"]])
    total = add_block(h, total, at_end, ("near", [h["across"]]), weight, layout)
    h["lent_d"] = lent_d
    fence(h)
    lent_c = swap_inside(h["lent"], "inner")
    h["lent_c"] = lent_c
    fence(h)
    lent_yc = swap_inside(h["lent_y"], "inner")
    h["lent_yc"], h["beyond0"], h["inner1"] = lent_yc, beyond0, inner1
    fence(h)
    beyond1 = hop_middle(h["inner1"])
    fence(h)
    lent_xc, lent_dc = swap_inside(h["lent_x"], "inner"), swap_inside(h["lent_d"], "inner")
    h["pair_m"] = pair_m
    fence(h)
    h["whole"] = added(h, h["pair"], h["pair_m"])
    h["lent_xc"], h["lent_dc"] = lent_xc, lent_dc
    fence(h)
    low_o = hop(h["whole"], OUTWARD)
    fence(h)
    up_x = swap(h["up"], "pool")
    fence(h)
    names = ("lent", "lent_c", "lent_x", "lent_xc", "lent_y", "lent_yc", "lent_d", "lent_dc")
    pieces = [h[n] for n in names]
    h["help0"] = helped(h, h["beyond0"], pieces, layout, 0)
    fence(h)
    help_o0 = hop(h["help0"], OUTWARD)
    fence(h)
    halves = [h["inner0"], h["inner1"]]
    total = add_block(h, total, None, ("partner", halves), weight, layout)
    h["relayed"], h["beyond1"], h["up_x"], h["low_o"] = relayed, beyond1, up_x, low_o
    fence(h)
    up_xc, up_c = swap(h["up_x"], "inner"), swap(h["up"], "inner")
    fence(h)
    pieces = [h[n] for n in names]
    h["help1"] = helped(h, h["beyond1"], pieces, layout, 1)
    h["up_xc"], h["up_c"] = up_xc, up_c
    fence(h)
    help_o1 = hop(h["help1"], OUTWARD)
    h["help_o0"] = help_o0
    fence(h)
    out, late = add_last(
        h,
        total,
        [h["low_o"], h["whole"]],
        h["use"],
        [h["up"], h["up_c"], h["up_x"], h["up_xc"]],
        h["relayed"],
        [h["beyond0"], h["beyond1"]],
        h["help_o0"],
        weight,
        layout,
    )
    h["help_o1"] = help_o1
    fence(h)
    return finished(h, out, late, h.pop("help_o1"), layout)


def owner_mask(slot, rank, adapters):
    which = slot[:, None, None] == jnp.arange(adapters, dtype=jnp.int32)[None, :, None]
    within = jnp.arange(MAXIMUM_RANK, dtype=jnp.int32)[None, None, :] < rank[:, None, None]
    return jnp.logical_and(which, within)


def gathered(tokens, tables, weight, down, up):
    slot, rank = slot_and_rank(*tables)
    axes = ("pool", "inner")
    base = jnp.dot(
        lax.all_gather(tokens, "tensor", axis=1, tiled=True),
        weight,
        preferred_element_type=jnp.float32,
    )
    downs = lax.all_gather(down, axes, axis=0, tiled=True)
    ups = lax.all_gather(up, axes, axis=0, tiled=True)
    mask = owner_mask(slot, rank, downs.shape[0])
    coords = lax.dot_general(
        tokens,
        downs.reshape(-1, downs.shape[2]),
        (((1,), (1,)), ((), ())),
        preferred_element_type=jnp.float32,
    ).reshape(mask.shape)
    coords = jnp.sum(jnp.where(mask, coords, 0.0), axis=1)
    low_rank = lax.psum(coords, "tensor").astype(jnp.bfloat16)
    spread = jnp.where(mask, low_rank[:, None, :], jnp.zeros((), jnp.bfloat16))
    delta = jnp.dot(
        spread.reshape(spread.shape[0], -1),
        ups.reshape(-1, ups.shape[2]),
        preferred_element_type=jnp.float32,
    ).astype(jnp.bfloat16)
    return (base + delta.astype(jnp.float32)).astype(jnp.bfloat16)


def shards(
    tokens,
    token_adapter_ids,
    adapter_pool_slot,
    adapter_rank_blocks,
    query_weight,
    pool_down_factors,
    pool_up_factors,
):
    tables = (token_adapter_ids, adapter_pool_slot, adapter_rank_blocks)
    whole_chain = tuple(lax.axis_size(a) for a in AXES) == (2, 4, 2, 2)
    run = chained if whole_chain else gathered
    return run(tokens, tables, query_weight, pool_down_factors, pool_up_factors)


def solution(mesh):
    in_specs = (
        P(("groups", "pool", "inner"), "tensor"),
        P(("groups", "pool", "inner")),
        P("groups"),
        P("groups"),
        P(None, "tensor"),
        P(("groups", "pool", "inner"), None, "tensor"),
        P(("groups", "pool", "inner"), None, "tensor"),
    )
    out_specs = P(("groups", "pool", "inner"), "tensor")
    return jax.shard_map(shards, mesh=mesh, in_specs=in_specs, out_specs=out_specs, check_vma=False)
```

```python
import itertools

import jax
import jax.numpy as jnp
import numpy as np
from jax import lax
from jax.experimental import pallas as pl
from jax.experimental.pallas import tpu as pltpu
from jax.sharding import PartitionSpec as P

MAXIMUM_RANK = 128
RBLK = 16
AXES = ("groups", "tensor", "pool", "inner")

PAIRS = [(0, 1), (1, 0), (2, 3), (3, 2)]
OUTWARD = [(1, 0), (2, 3)]


def lookup(indices, table):
    count = table.shape[0]
    match = indices[..., None] == jnp.arange(count, dtype=jnp.int32)
    return jnp.sum(jnp.where(match, table, 0), axis=-1)


def slot_and_rank(ids, slots, blocks):
    return lookup(ids, slots), RBLK * lookup(ids, blocks)


def swap(x, axis):
    return lax.ppermute(x, axis, [(0, 1), (1, 0)])


def inside(x, step):
    shape = (2, 4, 2, 2)
    pairs = []
    for place in itertools.product(*map(range, shape)):
        groups, z, pool, inner = place
        to = step(*place) if z in (1, 2) else (groups, z, pool, 1 - inner)
        pairs.append(tuple(int(np.ravel_multi_index(p, shape)) for p in (place, to)))
    return lax.ppermute(x, AXES, pairs)


def hop_middle(x):
    return inside(x, lambda g, z, p, i: (g, 3 - z, p, i))


def swap_inside(x, axis):
    steps = {
        "groups": lambda g, z, p, i: (1 - g, z, p, i),
        "pool": lambda g, z, p, i: (g, z, 1 - p, i),
        "inner": lambda g, z, p, i: (g, z, p, 1 - i),
    }
    return inside(x, steps[axis])


def hop(x, pairs):
    return lax.ppermute(x, "tensor", pairs)


VMEM = pl.BlockSpec(memory_space=pltpu.VMEM)
ANY = pl.BlockSpec(memory_space=pl.ANY)
HBM = pl.BlockSpec(memory_space=pltpu.HBM)


def call(held, body, out_shapes, operands, in_specs, out_specs=None, scratch=(), room=16, alias=None):
    single = not isinstance(out_shapes, list)
    shapes = [out_shapes] if single else out_shapes
    out_specs = out_specs or [VMEM] * len(shapes)
    ins, outs = len(operands), len(shapes)
    tick = held["tick"]

    def counted(*refs):
        into = refs[ins + 1 + outs]
        into[...] = refs[ins][...] + 1.0
        body(*refs[:ins], *refs[ins + 1 : ins + 1 + outs], *refs[ins + 2 + outs :])

    *results, held["tick"] = pl.pallas_call(
        counted,
        out_shape=[*shapes, jax.ShapeDtypeStruct(tick.shape, tick.dtype)],
        in_specs=[*in_specs, VMEM],
        out_specs=[*out_specs, VMEM],
        scratch_shapes=list(scratch),
        input_output_aliases=alias or {},
        cost_estimate=pl.CostEstimate(flops=10**12, bytes_accessed=0, transcendentals=0),
        compiler_params=pltpu.CompilerParams(vmem_limit_bytes=room << 20),
    )(*operands, tick)
    return results[0] if single else results


def fence(held):
    call(held, lambda: None, [], [], [])
    names = sorted(held)
    held.update(zip(names, lax.optimization_barrier(tuple(held[n] for n in names))))


def array(*shape, dtype=jnp.bfloat16):
    return jax.ShapeDtypeStruct(shape, dtype)


def dot(a, b):
    return jnp.dot(a, b, preferred_element_type=jnp.float32)


class Place:
    def __init__(self):
        z = lax.axis_index("tensor")
        self.own, self.partner = z, z ^ 1
        self.end = jnp.logical_or(z == 0, z == 3)
        self.near = jnp.where(self.end, 3 - self.partner, 3 - z)
        self.far = jnp.where(self.end, 3 - z, 3 - self.partner)
        self.seat = lax.axis_index(("groups", "pool", "inner"))
        self.mine = lax.axis_index(("pool", "inner"))


class Layout:
    def __init__(self, tokens, weight):
        self.tall, self.width = tokens.shape
        self.columns = weight.shape[1]
        self.deep = self.width // 8
        self.rows = self.deep // 2
        self.cut = self.tall - self.rows
        self.sizes = [self.cut, self.tall - self.cut]

    def sides(self, ref):
        for side in range(2):
            columns = pl.ds(side * self.columns, self.columns)
            yield side * self.rows, ref.at[:, columns]


def run_copies(copies):
    for copy in copies:
        copy.start()
    for copy in copies:
        copy.wait()


LARGE = 50


def first_rows(held, tokens, weight, layout):
    rows = layout.rows

    def body(t_ref, w_ref, out_ref, sem):
        place = Place()

        @pl.when(place.end)
        def _():
            start = place.far * layout.width + place.seat * layout.deep
            run_copies(
                [
                    pltpu.make_async_copy(
                        w_ref.at[pl.ds(pl.multiple_of(start + first, rows), rows)],
                        into,
                        sem.at[i],
                    )
                    for i, (first, into) in enumerate(layout.sides(out_ref))
                ]
            )

        @pl.when(jnp.logical_not(place.end))
        def _():
            run_copies(
                [pltpu.make_async_copy(t_ref.at[pl.ds(0, rows)], out_ref, sem.at[0])]
            )

    return call(
        held,
        body,
        array(rows, layout.width),
        [tokens, weight],
        [HBM, HBM],
        scratch=[pltpu.SemaphoreType.DMA((2,))],
        room=LARGE,
    )


def later_rows(held, tokens, layout):
    rows, cut = layout.rows, layout.cut

    def body(t_ref, out_ref, sem):
        start = pl.multiple_of(jnp.where(Place().end, 0, rows), rows)
        run_copies([pltpu.make_async_copy(t_ref.at[pl.ds(start, cut)], out_ref, sem)])

    return call(
        held,
        body,
        array(cut, layout.width),
        [tokens],
        [ANY],
        scratch=[pltpu.SemaphoreType.DMA],
    )


TALL = 32


def last_rows(held, tokens, across, coords, layout):
    cut, last = layout.sizes
    size, wide = last + TALL, coords.shape[1]
    count = layout.tall // TALL

    def body(t_ref, a_ref, c_ref, out_ref, rest_ref, sem):
        place = Place()
        rest = started(
            pltpu.make_async_copy(
                a_ref.at[pl.ds(size, layout.tall - size)], rest_ref, sem.at[0]
            )
        )

        @pl.when(place.end)
        def _():
            copy = pltpu.make_async_copy(
                t_ref.at[pl.ds(cut, last)], out_ref.at[pl.ds(0, last)], sem.at[1]
            )
            copy.start()
            for i in range(layout.width // wide):
                some = jnp.zeros((TALL, wide), out_ref.dtype)
                if i < count:
                    some = c_ref[i * TALL : (i + 1) * TALL, :].astype(out_ref.dtype)
                out_ref[last:, i * wide : (i + 1) * wide] = some
            copy.wait()

        @pl.when(jnp.logical_not(place.end))
        def _():
            run_copies(
                [pltpu.make_async_copy(a_ref.at[pl.ds(0, size)], out_ref, sem.at[1])]
            )

        waited(rest)

    return call(
        held,
        body,
        [array(size, layout.width), array(layout.tall - size, layout.width)],
        [tokens, across, coords],
        [ANY, ANY, VMEM],
        scratch=[pltpu.SemaphoreType.DMA((2,))],
    )


def unpacked(held, coords, x, layout):
    last, wide = layout.sizes[1], coords.shape[1]

    def body(c_ref, x_ref, out_ref, rows_ref, below_ref, sem):
        copies = started(
            pltpu.make_async_copy(x_ref.at[pl.ds(last, TALL)], below_ref, sem.at[0]),
            pltpu.make_async_copy(x_ref.at[pl.ds(0, last)], rows_ref, sem.at[1]),
        )
        copies[0].wait()
        for i in range(layout.tall // TALL):
            some = pl.ds(i * TALL, TALL)
            other = below_ref[:, i * wide : (i + 1) * wide].astype(jnp.float32)
            out_ref[some, :] = (c_ref[some, :] + other).astype(out_ref.dtype)
        copies[1].wait()

    return call(
        held,
        body,
        [array(*coords.shape), array(last, layout.width)],
        [coords, x],
        [VMEM, ANY],
        scratch=[
            pltpu.VMEM((TALL, layout.width), jnp.bfloat16),
            pltpu.SemaphoreType.DMA((2,)),
        ],
    )


PARTS = 4


class Rows:
    def __init__(self, x_ref, start, held_ref, sem, begin=True):
        self.depth, self.held_ref, self.copies = held_ref.shape[0] // PARTS, held_ref, []
        for i in range(PARTS):
            some = pl.ds(pl.multiple_of(start + i * self.depth, 128), self.depth)
            self.copies.append(
                pltpu.make_async_copy(
                    x_ref.at[some], held_ref.at[pl.ds(i * self.depth, self.depth)], sem.at[i]
                )
            )
        if begin:
            started(*self.copies)

    def dot(self, a_ref):
        total = 0.0
        for i, copy in enumerate(self.copies):
            copy.wait()
            some = pl.ds(i * self.depth, self.depth)
            total += dot(a_ref[:, some], self.held_ref[some, :])
        return total


def started(*copies):
    for copy in copies:
        copy.start()
    return copies


def waited(copies):
    for copy in copies:
        copy.wait()


def room(count, layout):
    shape = (layout.width, layout.columns)
    return [
        x
        for _ in range(count)
        for x in (pltpu.VMEM(shape, jnp.bfloat16), pltpu.SemaphoreType.DMA((PARTS,)))
    ]


def sums(layout):
    return array(layout.tall, layout.columns, dtype=jnp.float32)


def sums_room(layout):
    return [
        pltpu.VMEM((layout.tall, layout.columns), jnp.float32),
        pltpu.SemaphoreType.DMA((10,)),
    ]


def own_block(held, tokens, weight, layout):
    def body(a_ref, w_ref, out_ref, held_ref, w_sem, a_held, sum_ref, sem):
        load = started(pltpu.make_async_copy(a_ref, a_held, sem.at[0]))
        w = Rows(w_ref, Place().own * layout.width, held_ref, w_sem)
        waited(load)
        sum_ref[...] = w.dot(a_held)
        run_copies([pltpu.make_async_copy(sum_ref, out_ref, sem.at[1])])

    return call(
        held,
        body,
        sums(layout),
        [tokens, weight],
        [ANY, HBM],
        [HBM],
        room(1, layout)
        + [pltpu.VMEM((layout.tall, layout.width), jnp.bfloat16)]
        + sums_room(layout),
        room=LARGE,
    )


def add_block(held, total, at_end, inside, weight, layout):
    width, tall = layout.width, layout.tall
    arrays = [*at_end[1], *inside[1]]

    def body(total_ref, w_ref, *refs):
        array_refs = list(refs[: len(arrays)])
        out_ref, w_held, w_sem, a_held, sum_ref, sem = refs[len(arrays) :]
        place = Place()

        def run(name, part_refs):
            w = Rows(w_ref, getattr(place, name) * width, w_held, w_sem)
            loads, start = [], 0
            for i, ref in enumerate(part_refs):
                into = a_held.at[pl.ds(start, ref.shape[0])]
                loads.append(pltpu.make_async_copy(ref, into, sem.at[i]))
                start += ref.shape[0]
            started(*loads)
            more = started(pltpu.make_async_copy(total_ref, sum_ref, sem.at[3]))
            waited(loads)
            some = w.dot(a_held)
            waited(more)
            sum_ref[...] += some
            run_copies([pltpu.make_async_copy(sum_ref, out_ref, sem.at[4])])

        for side, here in ((at_end, place.end), (inside, jnp.logical_not(place.end))):
            mine = [array_refs.pop(0) for _ in side[1]]
            pl.when(here)(lambda side=side, mine=mine: run(side[0], mine))

    return call(
        held,
        body,
        sums(layout),
        [total, weight, *arrays],
        [HBM, HBM] + [ANY] * len(arrays),
        [HBM],
        room(1, layout) + [pltpu.VMEM((tall, width), jnp.bfloat16)] + sums_room(layout),
        room=LARGE,
    )


def add_last(held, total, low, use, ups, relayed, beyond, inner, weight, layout):
    adapters, rank, columns = ups[0].shape
    count = len(ups)
    cut, last = layout.sizes
    tall, width = layout.tall, layout.width

    def body(hop_ref, low_ref, use_ref, *refs):
        up_refs = refs[:count]
        total_ref, n0_ref, n1_ref, b0_ref, b1_ref, p0_ref, p1_ref, w_ref = refs[
            count : count + 8
        ]
        out_ref, sums_ref, *scratch = refs[count + 8 :]
        w_held, w_sem, v_held, v_sem, a_held, p_held, u_held, rows_ref, sum_ref, sem = scratch
        place = Place()
        first = n0_ref.shape[0]
        at_end = [
            pltpu.make_async_copy(n0_ref, a_held.at[pl.ds(0, first)], sem.at[0]),
            pltpu.make_async_copy(n1_ref, a_held.at[pl.ds(first, tall - first)], sem.at[1]),
        ]
        inside = [
            pltpu.make_async_copy(b0_ref, a_held.at[pl.ds(0, cut)], sem.at[0]),
            pltpu.make_async_copy(b1_ref, a_held.at[pl.ds(cut, last)], sem.at[1]),
        ]
        second = [
            pltpu.make_async_copy(p0_ref, p_held.at[pl.ds(0, cut)], sem.at[8]),
            pltpu.make_async_copy(
                p1_ref.at[pl.ds(0, last)], p_held.at[pl.ds(cut, last)], sem.at[9]
            ),
        ]

        loads = started(
            *[
                pltpu.make_async_copy(
                    up_ref,
                    u_held.at[pl.ds(i * adapters * rank, adapters * rank)],
                    sem.at[i + 3],
                )
                for i, up_ref in enumerate(up_refs)
            ],
            pltpu.make_async_copy(total_ref, sum_ref, sem.at[2]),
        )

        @pl.when(place.end)
        def _():
            started(*at_end)

        @pl.when(jnp.logical_not(place.end))
        def _():
            started(*inside)

        w = Rows(w_ref, jnp.where(place.end, place.near, place.far) * width, w_held, w_sem)
        v = Rows(w_ref, place.partner * width, v_held, v_sem, begin=False)

        @pl.when(jnp.logical_not(place.end))
        def _():
            started(*second, *v.copies)

        low = jnp.where(place.end, hop_ref[...], low_ref[...])
        some = [
            jnp.where(use_ref[...] == (place.mine ^ turn) * adapters + j, low, 0)
            for turn in range(count)
            for j in range(adapters)
        ]
        spread = jnp.concatenate(some, axis=1)
        waited(loads)
        terms = dot(spread, u_held[...])
        sum_ref[...] += terms.astype(jnp.bfloat16).astype(jnp.float32)

        @pl.when(place.end)
        def _():
            waited(at_end)

        @pl.when(jnp.logical_not(place.end))
        def _():
            waited(inside)

        sum_ref[...] += w.dot(a_held)

        @pl.when(place.end)
        def _():
            run_copies([pltpu.make_async_copy(sum_ref, sums_ref, sem.at[7])])

        @pl.when(jnp.logical_not(place.end))
        def _():
            waited(second)
            rows_ref[...] = (sum_ref[...] + v.dot(p_held)).astype(rows_ref.dtype)
            run_copies([pltpu.make_async_copy(rows_ref, out_ref, sem.at[7])])

    return call(
        held,
        body,
        [array(tall, columns), sums(layout)],
        [*low, use, *[u.reshape(-1, columns) for u in ups]]
        + [total, *relayed, *beyond, *inner, weight],
        [VMEM] * 3 + [ANY] * count + [HBM] + [ANY] * 6 + [HBM],
        [ANY, ANY],
        room(2, layout)
        + [
            pltpu.VMEM((tall, width), jnp.bfloat16),
            pltpu.VMEM((tall, width), jnp.bfloat16),
            pltpu.VMEM((count * adapters * rank, columns), jnp.bfloat16),
            pltpu.VMEM((tall, columns), jnp.bfloat16),
        ]
        + sums_room(layout),
        room=LARGE,
    )


def helped(held, beyond, pieces, layout, i):
    size, width, columns = layout.sizes[i], layout.width, layout.columns
    count, deep = len(pieces), layout.deep

    def body(beyond_ref, *refs):
        piece_refs = refs[:count]
        out_ref, b_held, w_held, sem = refs[count:]
        seat = Place().seat
        load = started(pltpu.make_async_copy(beyond_ref, b_held, sem.at[0]))
        lends = started(
            *[
                pltpu.make_async_copy(
                    part,
                    w_held.at[pl.ds(k * deep + first, layout.rows)],
                    sem.at[1 + 2 * k + side],
                )
                for k, piece_ref in enumerate(piece_refs)
                for side, (first, part) in enumerate(layout.sides(piece_ref))
            ]
        )
        waited(load)
        total = 0.0
        step = count // 4
        for first in range(0, count, step):
            blocks = [
                b_held[:, pl.ds(pl.multiple_of((seat ^ k) * deep, deep), deep)]
                for k in range(first, first + step)
            ]
            waited(lends[2 * first : 2 * (first + step)])
            some = w_held[first * deep : (first + step) * deep, :]
            total += dot(jnp.concatenate(blocks, axis=1), some)
        out_ref[...] = total.astype(out_ref.dtype)

    return call(
        held,
        body,
        array(size, columns),
        [beyond, *pieces],
        [ANY] * (1 + count),
        scratch=[
            pltpu.VMEM((size, width), jnp.bfloat16),
            pltpu.VMEM((width, columns), jnp.bfloat16),
            pltpu.SemaphoreType.DMA((1 + 2 * count,)),
        ],
    )


NOT_KEPT = ("tick", "tokens", "down", "up", "use")


def finished(held, out, total, term, i, layout, keep=False):
    start, size = i * layout.cut, layout.sizes[i]
    kept = [held[n] for n in sorted(held) if keep and n not in NOT_KEPT]

    def body(out_ref, total_ref, term_ref, *refs):
        into_ref, sum_ref, term_held, rows_ref, sem = refs[-5:]

        @pl.when(Place().end)
        def _():
            loads = started(
                pltpu.make_async_copy(total_ref.at[pl.ds(start, size)], sum_ref, sem.at[0]),
                pltpu.make_async_copy(term_ref, term_held, sem.at[1]),
            )
            waited(loads)
            rows_ref[...] = (sum_ref[...] + term_held[...].astype(jnp.float32)).astype(
                rows_ref.dtype
            )
            run_copies(
                [pltpu.make_async_copy(rows_ref, into_ref.at[pl.ds(start, size)], sem.at[2])]
            )

    return call(
        held,
        body,
        array(layout.tall, layout.columns),
        [out, total, term, *kept],
        [ANY] * (3 + len(kept)),
        [ANY],
        [
            pltpu.VMEM((size, layout.columns), jnp.float32),
            pltpu.VMEM((size, layout.columns), jnp.bfloat16),
            pltpu.VMEM((size, layout.columns), jnp.bfloat16),
            pltpu.SemaphoreType.DMA((3,)),
        ],
        alias={0: 0},
    )


def coords_of(held, tokens, use, downs, turns, before=None):
    adapters, rank = downs[0].shape[0], downs[0].shape[1]
    count = len(downs)

    def body(use_ref, tokens_ref, *refs):
        out_ref, sent_ref = refs[-2:]
        mine = Place().mine
        total = refs[count][...] if before is not None else 0.0
        for turn, down_ref in zip(turns, refs[:count]):
            coords = lax.dot_general(
                tokens_ref[...],
                down_ref[...],
                (((1,), (1,)), ((), ())),
                preferred_element_type=jnp.float32,
            )
            for j in range(adapters):
                some = coords[:, j * rank : (j + 1) * rank]
                mask = use_ref[...] == (mine ^ turn) * adapters + j
                total = total + jnp.where(mask, some, 0.0)
        out_ref[...] = total
        sent_ref[...] = total.astype(sent_ref.dtype)

    flat = [d.reshape(-1, d.shape[2]) for d in downs]
    more = [] if before is None else [before]
    shape = (tokens.shape[0], rank)
    return call(
        held,
        body,
        [array(*shape, dtype=jnp.float32), array(*shape)],
        [use, tokens, *flat, *more],
        [VMEM] * (2 + count + len(more)),
    )


def added(held, a, b):
    def body(a_ref, b_ref, out_ref):
        sums = a_ref[...].astype(jnp.float32) + b_ref[...].astype(jnp.float32)
        out_ref[...] = sums.astype(out_ref.dtype)

    return call(held, body, array(*a.shape), [a, b], [VMEM] * 2)


def chained(tokens, tables, weight, down, up):
    layout = Layout(tokens, weight)
    across = hop_middle(tokens)
    h = dict(tick=jnp.zeros((8, 128), jnp.float32), down=down, up=up, tokens=tokens)
    h["ids"], h["slots"], h["blocks"] = tables
    h["first"] = first_rows(h, tokens, weight, layout)
    fence(h)
    first_p = hop(h["first"], PAIRS)
    fence(h)
    down_c = swap(h["down"], "inner")
    fence(h)
    down_x = swap(h["down"], "pool")
    fence(h)
    h["later"] = later_rows(h, h["tokens"], layout)
    h["down_c"] = down_c
    fence(h)
    later_p = hop(h["later"], PAIRS)
    fence(h)
    slot, rank = slot_and_rank(h.pop("ids"), h.pop("slots"), h.pop("blocks"))
    row = jnp.arange(MAXIMUM_RANK, dtype=jnp.int32)[None, :]
    h["use"] = jnp.where(row < rank[:, None], slot[:, None], -1)
    total = own_block(h, h["tokens"], weight, layout)
    h["lent"] = first_p
    fence(h)
    lent_y = swap_inside(h["lent"], "groups")
    fence(h)
    coords, _ = coords_of(h, h["tokens"], h["use"], [h["down"], h["down_c"]], [0, 1])
    h["down_x"] = down_x
    fence(h)
    lent_x = swap_inside(h["lent"], "pool")
    fence(h)
    down_xc = swap(h["down_x"], "inner")
    fence(h)
    coords, _ = coords_of(h, h["tokens"], h["use"], [h["down_x"]], [2], coords)
    h["down_xc"] = down_xc
    fence(h)
    coords, _ = coords_of(h, h["tokens"], h["use"], [h["down_xc"]], [3], coords)
    h["across"] = across
    fence(h)
    h["last"], h["others"] = last_rows(h, h["tokens"], h["across"], coords, layout)
    h["later_p"], h["lent_y"] = later_p, lent_y
    fence(h)
    last_p = hop(h["last"], PAIRS)
    fence(h)
    beyond0 = hop_middle(h["later_p"])
    h["lent_x"] = lent_x
    fence(h)
    lent_d = swap_inside(h["lent_x"], "groups")
    fence(h)
    lent_c = swap_inside(h["lent"], "inner")
    fence(h)
    lent_yc = swap_inside(h["lent_y"], "inner")
    fence(h)
    at_end = ("partner", [h["lent"], h["later_p"]])
    total = add_block(h, total, at_end, ("near", [h["across"]]), weight, layout)
    h["lent_c"], h["lent_yc"] = lent_c, lent_yc
    fence(h)
    others_o = hop(h["others"], OUTWARD)
    fence(h)
    lent_xc = swap_inside(h["lent_x"], "inner")
    h["lent_xc"], h["lent_d"] = lent_xc, lent_d
    fence(h)
    lent_dc = swap_inside(h["lent_d"], "inner")
    h["lent_dc"], h["last_p"] = lent_dc, last_p
    fence(h)
    h["pair"], h["last_in"] = unpacked(h, coords, h["last_p"], layout)
    fence(h)
    pair_m = hop_middle(h["pair"])
    fence(h)
    beyond1 = hop_middle(h["last_in"])
    fence(h)
    up_x = swap(h["up"], "pool")
    h["beyond0"] = beyond0
    fence(h)
    names = ("lent", "lent_c", "lent_x", "lent_xc", "lent_y", "lent_yc", "lent_d", "lent_dc")
    pieces = [h[n] for n in names]
    h["help0"] = helped(h, h["beyond0"], pieces, layout, 0)
    h["pair_m"] = pair_m
    fence(h)
    h["whole"] = added(h, h["pair"], h["pair_m"])
    fence(h)
    low_o = hop(h["whole"], OUTWARD)
    fence(h)
    help_o0 = hop(h["help0"], OUTWARD)
    h["beyond1"], h["others_o"], h["up_x"] = beyond1, others_o, up_x
    fence(h)
    up_xc, up_c = swap(h["up_x"], "inner"), swap(h["up"], "inner")
    fence(h)
    pieces = [h[n] for n in names]
    h["help1"] = helped(h, h["beyond1"], pieces, layout, 1)
    h["up_xc"], h["up_c"] = up_xc, up_c
    fence(h)
    help_o1 = hop(h["help1"], OUTWARD)
    h["low_o"] = low_o
    fence(h)
    out, total = add_last(
        h,
        total,
        [h["low_o"], h["whole"]],
        h["use"],
        [h["up"], h["up_c"], h["up_x"], h["up_xc"]],
        [h["last_p"], h["others_o"]],
        [h["beyond0"], h["beyond1"]],
        [h["later_p"], h["last_p"]],
        weight,
        layout,
    )
    fence(h)
    h["help_o0"] = help_o0
    fence(h)
    out = finished(h, out, total, h["help_o0"], 0, layout)
    fence(h)
    h["help_o1"] = help_o1
    fence(h)
    return finished(h, out, total, h.pop("help_o1"), 1, layout, keep=True)


def owner_mask(slot, rank, adapters):
    which = slot[:, None, None] == jnp.arange(adapters, dtype=jnp.int32)[None, :, None]
    within = jnp.arange(MAXIMUM_RANK, dtype=jnp.int32)[None, None, :] < rank[:, None, None]
    return jnp.logical_and(which, within)


def gathered(tokens, tables, weight, down, up):
    slot, rank = slot_and_rank(*tables)
    axes = ("pool", "inner")
    base = jnp.dot(
        lax.all_gather(tokens, "tensor", axis=1, tiled=True),
        weight,
        preferred_element_type=jnp.float32,
    )
    downs = lax.all_gather(down, axes, axis=0, tiled=True)
    ups = lax.all_gather(up, axes, axis=0, tiled=True)
    mask = owner_mask(slot, rank, downs.shape[0])
    coords = lax.dot_general(
        tokens,
        downs.reshape(-1, downs.shape[2]),
        (((1,), (1,)), ((), ())),
        preferred_element_type=jnp.float32,
    ).reshape(mask.shape)
    coords = jnp.sum(jnp.where(mask, coords, 0.0), axis=1)
    low_rank = lax.psum(coords, "tensor").astype(jnp.bfloat16)
    spread = jnp.where(mask, low_rank[:, None, :], jnp.zeros((), jnp.bfloat16))
    delta = jnp.dot(
        spread.reshape(spread.shape[0], -1),
        ups.reshape(-1, ups.shape[2]),
        preferred_element_type=jnp.float32,
    ).astype(jnp.bfloat16)
    return (base + delta.astype(jnp.float32)).astype(jnp.bfloat16)


def shards(
    tokens,
    token_adapter_ids,
    adapter_pool_slot,
    adapter_rank_blocks,
    query_weight,
    pool_down_factors,
    pool_up_factors,
):
    tables = (token_adapter_ids, adapter_pool_slot, adapter_rank_blocks)
    whole_chain = tuple(lax.axis_size(a) for a in AXES) == (2, 4, 2, 2)
    run = chained if whole_chain else gathered
    return run(tokens, tables, query_weight, pool_down_factors, pool_up_factors)


def solution(mesh):
    in_specs = (
        P(("groups", "pool", "inner"), "tensor"),
        P(("groups", "pool", "inner")),
        P("groups"),
        P("groups"),
        P(None, "tensor"),
        P(("groups", "pool", "inner"), None, "tensor"),
        P(("groups", "pool", "inner"), None, "tensor"),
    )
    out_specs = P(("groups", "pool", "inner"), "tensor")
    return jax.shard_map(shards, mesh=mesh, in_specs=in_specs, out_specs=out_specs, check_vma=False)
```

```python
import itertools

import jax
import jax.numpy as jnp
import numpy as np
from jax import lax
from jax.experimental import pallas as pl
from jax.experimental.pallas import tpu as pltpu
from jax.sharding import PartitionSpec as P

MAXIMUM_RANK = 128
RBLK = 16
AXES = ("groups", "tensor", "pool", "inner")

PAIRS = [(0, 1), (1, 0), (2, 3), (3, 2)]
OUTWARD = [(1, 0), (2, 3)]


def lookup(indices, table):
    count = table.shape[0]
    match = indices[..., None] == jnp.arange(count, dtype=jnp.int32)
    return jnp.sum(jnp.where(match, table, 0), axis=-1)


def slot_and_rank(ids, slots, blocks):
    return lookup(ids, slots), RBLK * lookup(ids, blocks)


def swap(x, axis):
    return lax.ppermute(x, axis, [(0, 1), (1, 0)])


def inside(x, step):
    shape = (2, 4, 2, 2)
    pairs = []
    for place in itertools.product(*map(range, shape)):
        groups, z, pool, inner = place
        to = step(*place) if z in (1, 2) else (groups, z, pool, 1 - inner)
        pairs.append(tuple(int(np.ravel_multi_index(p, shape)) for p in (place, to)))
    return lax.ppermute(x, AXES, pairs)


def hop_middle(x):
    return inside(x, lambda g, z, p, i: (g, 3 - z, p, i))


def swap_inside(x, axis):
    steps = {
        "groups": lambda g, z, p, i: (1 - g, z, p, i),
        "pool": lambda g, z, p, i: (g, z, 1 - p, i),
        "inner": lambda g, z, p, i: (g, z, p, 1 - i),
    }
    return inside(x, steps[axis])


def hop(x, pairs):
    return lax.ppermute(x, "tensor", pairs)


VMEM = pl.BlockSpec(memory_space=pltpu.VMEM)
ANY = pl.BlockSpec(memory_space=pl.ANY)
HBM = pl.BlockSpec(memory_space=pltpu.HBM)


def call(held, body, out_shapes, operands, in_specs, out_specs=None, scratch=(), room=16, alias=None):
    single = not isinstance(out_shapes, list)
    shapes = [out_shapes] if single else out_shapes
    out_specs = out_specs or [VMEM] * len(shapes)
    ins, outs = len(operands), len(shapes)
    tick = held["tick"]

    def counted(*refs):
        into = refs[ins + 1 + outs]
        into[...] = refs[ins][...] + 1.0
        body(*refs[:ins], *refs[ins + 1 : ins + 1 + outs], *refs[ins + 2 + outs :])

    *results, held["tick"] = pl.pallas_call(
        counted,
        out_shape=[*shapes, jax.ShapeDtypeStruct(tick.shape, tick.dtype)],
        in_specs=[*in_specs, VMEM],
        out_specs=[*out_specs, VMEM],
        scratch_shapes=list(scratch),
        input_output_aliases=alias or {},
        cost_estimate=pl.CostEstimate(flops=10**12, bytes_accessed=0, transcendentals=0),
        compiler_params=pltpu.CompilerParams(vmem_limit_bytes=room << 20),
    )(*operands, tick)
    return results[0] if single else results


def fence(held):
    call(held, lambda: None, [], [], [])
    names = sorted(held)
    held.update(zip(names, lax.optimization_barrier(tuple(held[n] for n in names))))


def array(*shape, dtype=jnp.bfloat16):
    return jax.ShapeDtypeStruct(shape, dtype)


def dot(a, b):
    return jnp.dot(a, b, preferred_element_type=jnp.float32)


class Place:
    def __init__(self):
        z = lax.axis_index("tensor")
        self.own, self.partner = z, z ^ 1
        self.end = jnp.logical_or(z == 0, z == 3)
        self.near = jnp.where(self.end, 3 - self.partner, 3 - z)
        self.far = jnp.where(self.end, 3 - z, 3 - self.partner)
        self.seat = lax.axis_index(("groups", "pool", "inner"))
        self.mine = lax.axis_index(("pool", "inner"))


class Layout:
    def __init__(self, tokens, weight):
        self.tall, self.width = tokens.shape
        self.columns = weight.shape[1]
        self.deep = self.width // 8
        self.rows = self.deep // 2
        self.cut = self.tall - self.rows
        self.sizes = [self.cut, self.tall - self.cut]

    def sides(self, ref):
        for side in range(2):
            columns = pl.ds(side * self.columns, self.columns)
            yield side * self.rows, ref.at[:, columns]


def run_copies(copies):
    for copy in copies:
        copy.start()
    for copy in copies:
        copy.wait()


LARGE = 50


def first_rows(held, tokens, weight, layout):
    rows = layout.rows

    def body(t_ref, w_ref, out_ref, sem):
        place = Place()

        @pl.when(place.end)
        def _():
            start = place.far * layout.width + place.seat * layout.deep
            run_copies(
                [
                    pltpu.make_async_copy(
                        w_ref.at[pl.ds(pl.multiple_of(start + first, rows), rows)],
                        into,
                        sem.at[i],
                    )
                    for i, (first, into) in enumerate(layout.sides(out_ref))
                ]
            )

        @pl.when(jnp.logical_not(place.end))
        def _():
            run_copies(
                [pltpu.make_async_copy(t_ref.at[pl.ds(0, rows)], out_ref, sem.at[0])]
            )

    return call(
        held,
        body,
        array(rows, layout.width),
        [tokens, weight],
        [HBM, HBM],
        scratch=[pltpu.SemaphoreType.DMA((2,))],
        room=LARGE,
    )


def later_rows(held, tokens, layout):
    rows, cut = layout.rows, layout.cut

    def body(t_ref, out_ref, sem):
        start = pl.multiple_of(jnp.where(Place().end, 0, rows), rows)
        run_copies([pltpu.make_async_copy(t_ref.at[pl.ds(start, cut)], out_ref, sem)])

    return call(
        held,
        body,
        array(cut, layout.width),
        [tokens],
        [ANY],
        scratch=[pltpu.SemaphoreType.DMA],
    )


TALL = 32


def last_rows(held, tokens, across, coords, layout):
    cut, last = layout.sizes
    size = last + TALL
    wide = coords.shape[1]
    count = layout.tall // TALL

    def body(t_ref, a_ref, c_ref, out_ref, sem):
        place = Place()

        @pl.when(place.end)
        def _():
            copy = pltpu.make_async_copy(
                t_ref.at[pl.ds(cut, last)], out_ref.at[pl.ds(0, last)], sem
            )
            copy.start()
            for i in range(layout.width // wide):
                some = jnp.zeros((TALL, wide), out_ref.dtype)
                if i < count:
                    some = c_ref[i * TALL : (i + 1) * TALL, :].astype(out_ref.dtype)
                out_ref[last:, i * wide : (i + 1) * wide] = some
            copy.wait()

        @pl.when(jnp.logical_not(place.end))
        def _():
            run_copies([pltpu.make_async_copy(a_ref.at[pl.ds(0, size)], out_ref, sem)])

    return call(
        held,
        body,
        array(size, layout.width),
        [tokens, across, coords],
        [ANY, ANY, VMEM],
        scratch=[pltpu.SemaphoreType.DMA],
    )


def other_rows(held, across, layout):
    size = layout.sizes[1] + TALL
    rest = layout.tall - size

    def body(a_ref, out_ref, sem):
        run_copies([pltpu.make_async_copy(a_ref.at[pl.ds(size, rest)], out_ref, sem)])

    return call(
        held,
        body,
        array(rest, layout.width),
        [across],
        [ANY],
        scratch=[pltpu.SemaphoreType.DMA],
    )


def unpacked(held, coords, x, layout):
    last, wide = layout.sizes[1], coords.shape[1]

    def body(c_ref, x_ref, out_ref, rows_ref, below_ref, sem):
        copies = started(
            pltpu.make_async_copy(x_ref.at[pl.ds(last, TALL)], below_ref, sem.at[0]),
            pltpu.make_async_copy(x_ref.at[pl.ds(0, last)], rows_ref, sem.at[1]),
        )
        copies[0].wait()
        for i in range(layout.tall // TALL):
            some = pl.ds(i * TALL, TALL)
            other = below_ref[:, i * wide : (i + 1) * wide].astype(jnp.float32)
            out_ref[some, :] = (c_ref[some, :] + other).astype(out_ref.dtype)
        copies[1].wait()

    return call(
        held,
        body,
        [array(*coords.shape), array(last, layout.width)],
        [coords, x],
        [VMEM, ANY],
        scratch=[
            pltpu.VMEM((TALL, layout.width), jnp.bfloat16),
            pltpu.SemaphoreType.DMA((2,)),
        ],
    )


PARTS = 4


class Rows:
    def __init__(self, x_ref, start, held_ref, sem, begin=True):
        self.depth, self.held_ref, self.copies = held_ref.shape[0] // PARTS, held_ref, []
        for i in range(PARTS):
            some = pl.ds(pl.multiple_of(start + i * self.depth, 128), self.depth)
            self.copies.append(
                pltpu.make_async_copy(
                    x_ref.at[some], held_ref.at[pl.ds(i * self.depth, self.depth)], sem.at[i]
                )
            )
        if begin:
            started(*self.copies)

    def dot(self, a_ref):
        total = 0.0
        for i, copy in enumerate(self.copies):
            copy.wait()
            some = pl.ds(i * self.depth, self.depth)
            total += dot(a_ref[:, some], self.held_ref[some, :])
        return total


def started(*copies):
    for copy in copies:
        copy.start()
    return copies


def waited(copies):
    for copy in copies:
        copy.wait()


def room(count, layout):
    shape = (layout.width, layout.columns)
    return [
        x
        for _ in range(count)
        for x in (pltpu.VMEM(shape, jnp.bfloat16), pltpu.SemaphoreType.DMA((PARTS,)))
    ]


def sums(layout):
    return array(layout.tall, layout.columns, dtype=jnp.float32)


def sums_room(layout):
    return [
        pltpu.VMEM((layout.tall, layout.columns), jnp.float32),
        pltpu.SemaphoreType.DMA((10,)),
    ]


def own_block(held, tokens, weight, layout):
    def body(a_ref, w_ref, out_ref, held_ref, w_sem, a_held, sum_ref, sem):
        load = started(pltpu.make_async_copy(a_ref, a_held, sem.at[0]))
        w = Rows(w_ref, Place().own * layout.width, held_ref, w_sem)
        waited(load)
        sum_ref[...] = w.dot(a_held)
        run_copies([pltpu.make_async_copy(sum_ref, out_ref, sem.at[1])])

    return call(
        held,
        body,
        sums(layout),
        [tokens, weight],
        [ANY, HBM],
        [HBM],
        room(1, layout)
        + [pltpu.VMEM((layout.tall, layout.width), jnp.bfloat16)]
        + sums_room(layout),
        room=LARGE,
    )


def add_block(held, total, at_end, inside, weight, layout):
    width, tall = layout.width, layout.tall
    arrays = [*at_end[1], *inside[1]]

    def body(total_ref, w_ref, *refs):
        array_refs = list(refs[: len(arrays)])
        out_ref, w_held, w_sem, a_held, sum_ref, sem = refs[len(arrays) :]
        place = Place()

        def run(name, part_refs):
            w = Rows(w_ref, getattr(place, name) * width, w_held, w_sem)
            loads, start = [], 0
            for i, ref in enumerate(part_refs):
                into = a_held.at[pl.ds(start, ref.shape[0])]
                loads.append(pltpu.make_async_copy(ref, into, sem.at[i]))
                start += ref.shape[0]
            started(*loads)
            more = started(pltpu.make_async_copy(total_ref, sum_ref, sem.at[3]))
            waited(loads)
            some = w.dot(a_held)
            waited(more)
            sum_ref[...] += some
            run_copies([pltpu.make_async_copy(sum_ref, out_ref, sem.at[4])])

        for side, here in ((at_end, place.end), (inside, jnp.logical_not(place.end))):
            mine = [array_refs.pop(0) for _ in side[1]]
            pl.when(here)(lambda side=side, mine=mine: run(side[0], mine))

    return call(
        held,
        body,
        sums(layout),
        [total, weight, *arrays],
        [HBM, HBM] + [ANY] * len(arrays),
        [HBM],
        room(1, layout) + [pltpu.VMEM((tall, width), jnp.bfloat16)] + sums_room(layout),
        room=LARGE,
    )


def spread_of(use, low, place, count, adapters):
    some = [
        jnp.where(use == (place.mine ^ turn) * adapters + j, low, 0)
        for turn in range(count)
        for j in range(adapters)
    ]
    return jnp.concatenate(some, axis=1)


def terms_of(spread, ups_held):
    return dot(spread, ups_held).astype(jnp.bfloat16).astype(jnp.float32)


def add_last(held, total, low, use, ups, relayed, beyond, inner, weight, layout):
    adapters, rank, columns = ups[0].shape
    count = len(ups)
    cut, last = layout.sizes
    tall, width = layout.tall, layout.width

    def body(low_ref, use_ref, *refs):
        up_refs = refs[:count]
        total_ref, n0_ref, n1_ref, b0_ref, b1_ref, p0_ref, p1_ref, w_ref = refs[
            count : count + 8
        ]
        out_ref, sums_ref, *scratch = refs[count + 8 :]
        w_held, w_sem, v_held, v_sem, a_held, p_held, u_held, rows_ref, sum_ref, sem = scratch
        place = Place()
        first = n0_ref.shape[0]
        load = pltpu.make_async_copy(total_ref, sum_ref, sem.at[2])
        load.start()

        @pl.when(place.end)
        def _():
            w = Rows(w_ref, place.near * width, w_held, w_sem)
            loads = started(
                pltpu.make_async_copy(n0_ref, a_held.at[pl.ds(0, first)], sem.at[0]),
                pltpu.make_async_copy(n1_ref, a_held.at[pl.ds(first, tall - first)], sem.at[1]),
            )
            waited(loads)
            load.wait()
            sum_ref[...] += w.dot(a_held)
            run_copies([pltpu.make_async_copy(sum_ref, sums_ref, sem.at[7])])

        @pl.when(jnp.logical_not(place.end))
        def _():
            loads = started(
                *[
                    pltpu.make_async_copy(
                        up_ref,
                        u_held.at[pl.ds(i * adapters * rank, adapters * rank)],
                        sem.at[i + 3],
                    )
                    for i, up_ref in enumerate(up_refs)
                ]
            )
            beyonds = started(
                pltpu.make_async_copy(b0_ref, a_held.at[pl.ds(0, cut)], sem.at[0]),
                pltpu.make_async_copy(b1_ref, a_held.at[pl.ds(cut, last)], sem.at[1]),
            )
            w = Rows(w_ref, place.far * width, w_held, w_sem)
            inners = started(
                pltpu.make_async_copy(p0_ref, p_held.at[pl.ds(0, cut)], sem.at[8]),
                pltpu.make_async_copy(
                    p1_ref.at[pl.ds(0, last)], p_held.at[pl.ds(cut, last)], sem.at[9]
                ),
            )
            v = Rows(w_ref, place.partner * width, v_held, v_sem)
            spread = spread_of(use_ref[...], low_ref[...], place, count, adapters)
            waited(loads)
            terms = terms_of(spread, u_held[...])
            load.wait()
            sum_ref[...] += terms
            waited(beyonds)
            sum_ref[...] += w.dot(a_held)
            waited(inners)
            rows_ref[...] = (sum_ref[...] + v.dot(p_held)).astype(rows_ref.dtype)
            run_copies([pltpu.make_async_copy(rows_ref, out_ref, sem.at[7])])

    return call(
        held,
        body,
        [array(tall, columns), sums(layout)],
        [low, use, *[u.reshape(-1, columns) for u in ups]]
        + [total, *relayed, *beyond, *inner, weight],
        [VMEM] * 2 + [ANY] * count + [HBM] + [ANY] * 6 + [HBM],
        [ANY, HBM],
        room(2, layout)
        + [
            pltpu.VMEM((tall, width), jnp.bfloat16),
            pltpu.VMEM((tall, width), jnp.bfloat16),
            pltpu.VMEM((count * adapters * rank, columns), jnp.bfloat16),
            pltpu.VMEM((tall, columns), jnp.bfloat16),
        ]
        + sums_room(layout),
        room=LARGE,
    )


def helped(held, beyond, pieces, layout, i):
    size, width, columns = layout.sizes[i], layout.width, layout.columns
    count, deep = len(pieces), layout.deep

    def body(beyond_ref, *refs):
        piece_refs = refs[:count]
        out_ref, b_held, w_held, sem = refs[count:]
        place = Place()
        seat = place.seat

        @pl.when(jnp.logical_not(place.end))
        def _():
            load = started(pltpu.make_async_copy(beyond_ref, b_held, sem.at[0]))
            lends = started(
                *[
                    pltpu.make_async_copy(
                        part,
                        w_held.at[pl.ds(k * deep + first, layout.rows)],
                        sem.at[1 + 2 * k + side],
                    )
                    for k, piece_ref in enumerate(piece_refs)
                    for side, (first, part) in enumerate(layout.sides(piece_ref))
                ]
            )
            waited(load)
            total = 0.0
            step = count // 4
            for first in range(0, count, step):
                blocks = [
                    b_held[:, pl.ds(pl.multiple_of((seat ^ k) * deep, deep), deep)]
                    for k in range(first, first + step)
                ]
                waited(lends[2 * first : 2 * (first + step)])
                some = w_held[first * deep : (first + step) * deep, :]
                total += dot(jnp.concatenate(blocks, axis=1), some)
            out_ref[...] = total.astype(out_ref.dtype)

    return call(
        held,
        body,
        array(size, columns),
        [beyond, *pieces],
        [ANY] * (1 + count),
        scratch=[
            pltpu.VMEM((size, width), jnp.bfloat16),
            pltpu.VMEM((width, columns), jnp.bfloat16),
            pltpu.SemaphoreType.DMA((1 + 2 * count,)),
        ],
    )


NOT_KEPT = ("tick", "tokens", "down", "up", "use")


def first_finished(held, out, total, term, low, use, ups, layout):
    adapters, rank, columns = ups[0].shape
    count = len(ups)
    cut, last = layout.sizes

    def body(out_ref, total_ref, term_ref, low_ref, use_ref, *refs):
        up_refs = refs[:count]
        into_ref, late_ref, sum_ref, term_held, u_held, rows_ref, low_held, use_held, sem = refs[
            count:
        ]
        place = Place()

        @pl.when(place.end)
        def _():
            first = started(
                pltpu.make_async_copy(low_ref, low_held, sem.at[count + 2]),
                pltpu.make_async_copy(use_ref, use_held, sem.at[count + 3]),
            )
            loads = started(
                *[
                    pltpu.make_async_copy(
                        up_ref,
                        u_held.at[pl.ds(i * adapters * rank, adapters * rank)],
                        sem.at[i],
                    )
                    for i, up_ref in enumerate(up_refs)
                ],
                pltpu.make_async_copy(total_ref, sum_ref, sem.at[count]),
                pltpu.make_async_copy(term_ref, term_held, sem.at[count + 1]),
            )
            waited(first)
            spread = spread_of(use_held[...], low_held[...], place, count, adapters)
            waited(loads)
            sum_ref[...] += terms_of(spread, u_held[...])
            stores = started(
                pltpu.make_async_copy(sum_ref.at[pl.ds(cut, last)], late_ref, sem.at[0])
            )
            rows_ref[...] = (sum_ref[:cut, :] + term_held[...].astype(jnp.float32)).astype(
                rows_ref.dtype
            )
            run_copies([pltpu.make_async_copy(rows_ref, into_ref.at[pl.ds(0, cut)], sem.at[1])])
            waited(stores)

    return call(
        held,
        body,
        [array(layout.tall, columns), array(last, columns, dtype=jnp.float32)],
        [out, total, term, low, use, *[u.reshape(-1, columns) for u in ups]],
        [ANY, HBM] + [ANY] * (3 + count),
        [ANY, ANY],
        [
            pltpu.VMEM((layout.tall, columns), jnp.float32),
            pltpu.VMEM((cut, columns), jnp.bfloat16),
            pltpu.VMEM((count * adapters * rank, columns), jnp.bfloat16),
            pltpu.VMEM((cut, columns), jnp.bfloat16),
            pltpu.VMEM(low.shape, low.dtype),
            pltpu.VMEM(use.shape, use.dtype),
            pltpu.SemaphoreType.DMA((count + 4,)),
        ],
        alias={0: 0},
    )


def last_finished(held, out, late, term, layout):
    kept = [held[n] for n in sorted(held) if n.startswith("lent")]
    cut, last = layout.sizes

    def body(out_ref, late_ref, term_ref, *refs):
        into_ref, late_held, term_held, rows_ref, sem = refs[-5:]

        @pl.when(Place().end)
        def _():
            run_copies(
                [
                    pltpu.make_async_copy(late_ref, late_held, sem.at[0]),
                    pltpu.make_async_copy(term_ref, term_held, sem.at[1]),
                ]
            )
            rows_ref[...] = (late_held[...] + term_held[...].astype(jnp.float32)).astype(
                rows_ref.dtype
            )
            run_copies(
                [pltpu.make_async_copy(rows_ref, into_ref.at[pl.ds(cut, last)], sem.at[2])]
            )

    return call(
        held,
        body,
        array(*out.shape),
        [out, late, term, *kept],
        [ANY] * (3 + len(kept)),
        [ANY],
        [
            pltpu.VMEM((last, layout.columns), jnp.float32),
            pltpu.VMEM((last, layout.columns), out.dtype),
            pltpu.VMEM((last, layout.columns), out.dtype),
            pltpu.SemaphoreType.DMA((3,)),
        ],
        alias={0: 0},
    )


def coords_of(held, tokens, use, downs, turns, before=None):
    adapters, rank = downs[0].shape[0], downs[0].shape[1]
    count = len(downs)

    def body(use_ref, tokens_ref, *refs):
        out_ref, sent_ref = refs[-2:]
        mine = Place().mine
        total = refs[count][...] if before is not None else 0.0
        for turn, down_ref in zip(turns, refs[:count]):
            coords = lax.dot_general(
                tokens_ref[...],
                down_ref[...],
                (((1,), (1,)), ((), ())),
                preferred_element_type=jnp.float32,
            )
            for j in range(adapters):
                some = coords[:, j * rank : (j + 1) * rank]
                mask = use_ref[...] == (mine ^ turn) * adapters + j
                total = total + jnp.where(mask, some, 0.0)
        out_ref[...] = total
        sent_ref[...] = total.astype(sent_ref.dtype)

    flat = [d.reshape(-1, d.shape[2]) for d in downs]
    more = [] if before is None else [before]
    shape = (tokens.shape[0], rank)
    return call(
        held,
        body,
        [array(*shape, dtype=jnp.float32), array(*shape)],
        [use, tokens, *flat, *more],
        [VMEM] * (2 + count + len(more)),
    )


def added(held, a, b):
    def body(a_ref, b_ref, out_ref):
        sums = a_ref[...].astype(jnp.float32) + b_ref[...].astype(jnp.float32)
        out_ref[...] = sums.astype(out_ref.dtype)

    return call(held, body, array(*a.shape), [a, b], [VMEM] * 2)


def chained(tokens, tables, weight, down, up):
    layout = Layout(tokens, weight)
    across = hop_middle(tokens)
    h = dict(tick=jnp.zeros((8, 128), jnp.float32), down=down, up=up, tokens=tokens)
    h["ids"], h["slots"], h["blocks"] = tables
    h["first"] = first_rows(h, tokens, weight, layout)
    fence(h)
    first_p = hop(h["first"], PAIRS)
    fence(h)
    down_c = swap(h["down"], "inner")
    fence(h)
    down_x = swap(h["down"], "pool")
    fence(h)
    h["later"] = later_rows(h, h["tokens"], layout)
    h["down_c"] = down_c
    fence(h)
    later_p = hop(h["later"], PAIRS)
    fence(h)
    slot, rank = slot_and_rank(h.pop("ids"), h.pop("slots"), h.pop("blocks"))
    row = jnp.arange(MAXIMUM_RANK, dtype=jnp.int32)[None, :]
    h["use"] = jnp.where(row < rank[:, None], slot[:, None], -1)
    total = own_block(h, h["tokens"], weight, layout)
    h["lent"] = first_p
    fence(h)
    lent_y = swap_inside(h["lent"], "groups")
    fence(h)
    coords, _ = coords_of(h, h["tokens"], h["use"], [h["down"], h["down_c"]], [0, 1])
    h["down_x"] = down_x
    fence(h)
    lent_x = swap_inside(h["lent"], "pool")
    fence(h)
    down_xc = swap(h["down_x"], "inner")
    fence(h)
    coords, _ = coords_of(h, h["tokens"], h["use"], [h["down_x"]], [2], coords)
    h["down_xc"] = down_xc
    fence(h)
    coords, _ = coords_of(h, h["tokens"], h["use"], [h["down_xc"]], [3], coords)
    h["across"] = across
    fence(h)
    h["last"] = last_rows(h, h["tokens"], h["across"], coords, layout)
    h["later_p"], h["lent_y"] = later_p, lent_y
    fence(h)
    last_p = hop(h["last"], PAIRS)
    fence(h)
    beyond0 = hop_middle(h["later_p"])
    h["lent_x"] = lent_x
    fence(h)
    lent_d = swap_inside(h["lent_x"], "groups")
    fence(h)
    lent_c = swap_inside(h["lent"], "inner")
    fence(h)
    lent_yc = swap_inside(h["lent_y"], "inner")
    fence(h)
    h["others"] = other_rows(h, h["across"], layout)
    h["lent_c"], h["lent_yc"] = lent_c, lent_yc
    fence(h)
    others_o = hop(h["others"], OUTWARD)
    fence(h)
    lent_xc = swap_inside(h["lent_x"], "inner")
    fence(h)
    at_end = ("partner", [h["lent"], h["later_p"]])
    total = add_block(h, total, at_end, ("near", [h["across"]]), weight, layout)
    h["lent_xc"], h["lent_d"] = lent_xc, lent_d
    fence(h)
    lent_dc = swap_inside(h["lent_d"], "inner")
    h["lent_dc"], h["last_p"] = lent_dc, last_p
    fence(h)
    h["pair"], h["last_in"] = unpacked(h, coords, h["last_p"], layout)
    fence(h)
    pair_m = hop_middle(h["pair"])
    fence(h)
    beyond1 = hop_middle(h["last_in"])
    fence(h)
    up_x = swap(h["up"], "pool")
    h["beyond0"] = beyond0
    fence(h)
    names = ("lent", "lent_c", "lent_x", "lent_xc", "lent_y", "lent_yc", "lent_d", "lent_dc")
    pieces = [h[n] for n in names]
    h["help0"] = helped(h, h["beyond0"], pieces, layout, 0)
    h["pair_m"] = pair_m
    fence(h)
    help_o0 = hop(h["help0"], OUTWARD)
    fence(h)
    h["whole"] = added(h, h["pair"], h["pair_m"])
    fence(h)
    low_o = hop(h["whole"], OUTWARD)
    h["beyond1"], h["others_o"], h["up_x"] = beyond1, others_o, up_x
    fence(h)
    up_xc, up_c = swap(h["up_x"], "inner"), swap(h["up"], "inner")
    fence(h)
    pieces = [h[n] for n in names]
    h["help1"] = helped(h, h["beyond1"], pieces, layout, 1)
    h["up_xc"], h["up_c"] = up_xc, up_c
    fence(h)
    help_o1 = hop(h["help1"], OUTWARD)
    fence(h)
    ups = [h["up"], h["up_c"], h["up_x"], h["up_xc"]]
    out, total = add_last(
        h,
        total,
        h["whole"],
        h["use"],
        ups,
        [h["last_p"], h["others_o"]],
        [h["beyond0"], h["beyond1"]],
        [h["later_p"], h["last_p"]],
        weight,
        layout,
    )
    fence(h)
    h["help_o0"], h["low_o"] = help_o0, low_o
    fence(h)
    ups = [h["up"], h["up_c"], h["up_x"], h["up_xc"]]
    out, late = first_finished(h, out, total, h["help_o0"], h["low_o"], h["use"], ups, layout)
    fence(h)
    h["help_o1"] = help_o1
    fence(h)
    return last_finished(h, out, late, h.pop("help_o1"), layout)


def owner_mask(slot, rank, adapters):
    which = slot[:, None, None] == jnp.arange(adapters, dtype=jnp.int32)[None, :, None]
    within = jnp.arange(MAXIMUM_RANK, dtype=jnp.int32)[None, None, :] < rank[:, None, None]
    return jnp.logical_and(which, within)


def gathered(tokens, tables, weight, down, up):
    slot, rank = slot_and_rank(*tables)
    axes = ("pool", "inner")
    base = jnp.dot(
        lax.all_gather(tokens, "tensor", axis=1, tiled=True),
        weight,
        preferred_element_type=jnp.float32,
    )
    downs = lax.all_gather(down, axes, axis=0, tiled=True)
    ups = lax.all_gather(up, axes, axis=0, tiled=True)
    mask = owner_mask(slot, rank, downs.shape[0])
    coords = lax.dot_general(
        tokens,
        downs.reshape(-1, downs.shape[2]),
        (((1,), (1,)), ((), ())),
        preferred_element_type=jnp.float32,
    ).reshape(mask.shape)
    coords = jnp.sum(jnp.where(mask, coords, 0.0), axis=1)
    low_rank = lax.psum(coords, "tensor").astype(jnp.bfloat16)
    spread = jnp.where(mask, low_rank[:, None, :], jnp.zeros((), jnp.bfloat16))
    delta = jnp.dot(
        spread.reshape(spread.shape[0], -1),
        ups.reshape(-1, ups.shape[2]),
        preferred_element_type=jnp.float32,
    ).astype(jnp.bfloat16)
    return (base + delta.astype(jnp.float32)).astype(jnp.bfloat16)


def shards(
    tokens,
    token_adapter_ids,
    adapter_pool_slot,
    adapter_rank_blocks,
    query_weight,
    pool_down_factors,
    pool_up_factors,
):
    tables = (token_adapter_ids, adapter_pool_slot, adapter_rank_blocks)
    whole_chain = tuple(lax.axis_size(a) for a in AXES) == (2, 4, 2, 2)
    run = chained if whole_chain else gathered
    return run(tokens, tables, query_weight, pool_down_factors, pool_up_factors)


def solution(mesh):
    in_specs = (
        P(("groups", "pool", "inner"), "tensor"),
        P(("groups", "pool", "inner")),
        P("groups"),
        P("groups"),
        P(None, "tensor"),
        P(("groups", "pool", "inner"), None, "tensor"),
        P(("groups", "pool", "inner"), None, "tensor"),
    )
    out_specs = P(("groups", "pool", "inner"), "tensor")
    return jax.shard_map(shards, mesh=mesh, in_specs=in_specs, out_specs=out_specs, check_vma=False)
```

```python
import itertools

import jax
import jax.numpy as jnp
import numpy as np
from jax import lax
from jax.experimental import pallas as pl
from jax.experimental.pallas import tpu as pltpu
from jax.sharding import PartitionSpec as P

MAXIMUM_RANK = 128
RBLK = 16
AXES = ("groups", "tensor", "pool", "inner")

PAIRS = [(0, 1), (1, 0), (2, 3), (3, 2)]
OUTWARD = [(1, 0), (2, 3)]


def lookup(indices, table):
    count = table.shape[0]
    match = indices[..., None] == jnp.arange(count, dtype=jnp.int32)
    return jnp.sum(jnp.where(match, table, 0), axis=-1)


def slot_and_rank(ids, slots, blocks):
    return lookup(ids, slots), RBLK * lookup(ids, blocks)


def swap(x, axis):
    return lax.ppermute(x, axis, [(0, 1), (1, 0)])


def inside(x, step):
    shape = (2, 4, 2, 2)
    pairs = []
    for place in itertools.product(*map(range, shape)):
        groups, z, pool, inner = place
        to = step(*place) if z in (1, 2) else (groups, z, pool, 1 - inner)
        pairs.append(tuple(int(np.ravel_multi_index(p, shape)) for p in (place, to)))
    return lax.ppermute(x, AXES, pairs)


def hop_middle(x):
    return inside(x, lambda g, z, p, i: (g, 3 - z, p, i))


def swap_inside(x, axis):
    steps = {
        "groups": lambda g, z, p, i: (1 - g, z, p, i),
        "pool": lambda g, z, p, i: (g, z, 1 - p, i),
        "inner": lambda g, z, p, i: (g, z, p, 1 - i),
    }
    return inside(x, steps[axis])


def hop(x, pairs):
    return lax.ppermute(x, "tensor", pairs)


VMEM = pl.BlockSpec(memory_space=pltpu.VMEM)
ANY = pl.BlockSpec(memory_space=pl.ANY)
HBM = pl.BlockSpec(memory_space=pltpu.HBM)


def call(held, body, out_shapes, operands, in_specs, out_specs=None, scratch=(), room=16, alias=None):
    single = not isinstance(out_shapes, list)
    shapes = [out_shapes] if single else out_shapes
    out_specs = out_specs or [VMEM] * len(shapes)
    ins, outs = len(operands), len(shapes)
    tick = held["tick"]

    def counted(*refs):
        into = refs[ins + 1 + outs]
        into[...] = refs[ins][...] + 1.0
        body(*refs[:ins], *refs[ins + 1 : ins + 1 + outs], *refs[ins + 2 + outs :])

    *results, held["tick"] = pl.pallas_call(
        counted,
        out_shape=[*shapes, jax.ShapeDtypeStruct(tick.shape, tick.dtype)],
        in_specs=[*in_specs, VMEM],
        out_specs=[*out_specs, VMEM],
        scratch_shapes=list(scratch),
        input_output_aliases=alias or {},
        cost_estimate=pl.CostEstimate(flops=10**12, bytes_accessed=0, transcendentals=0),
        compiler_params=pltpu.CompilerParams(vmem_limit_bytes=room << 20),
    )(*operands, tick)
    return results[0] if single else results


def fence(held):
    call(held, lambda: None, [], [], [])
    names = sorted(held)
    held.update(zip(names, lax.optimization_barrier(tuple(held[n] for n in names))))


def array(*shape, dtype=jnp.bfloat16):
    return jax.ShapeDtypeStruct(shape, dtype)


def dot(a, b):
    return jnp.dot(a, b, preferred_element_type=jnp.float32)


class Place:
    def __init__(self):
        z = lax.axis_index("tensor")
        self.own, self.partner = z, z ^ 1
        self.end = jnp.logical_or(z == 0, z == 3)
        self.near = jnp.where(self.end, 3 - self.partner, 3 - z)
        self.far = jnp.where(self.end, 3 - z, 3 - self.partner)
        self.seat = lax.axis_index(("groups", "pool", "inner"))
        self.mine = lax.axis_index(("pool", "inner"))


class Layout:
    def __init__(self, tokens, weight):
        self.tall, self.width = tokens.shape
        self.columns = weight.shape[1]
        self.deep = self.width // 8
        self.rows = self.deep // 2
        self.cut = self.tall - self.rows
        self.sizes = [self.cut, self.tall - self.cut]

    def sides(self, ref):
        for side in range(2):
            columns = pl.ds(side * self.columns, self.columns)
            yield side * self.rows, ref.at[:, columns]


def run_copies(copies):
    for copy in copies:
        copy.start()
    for copy in copies:
        copy.wait()


LARGE = 50


def first_rows(held, tokens, weight, layout):
    rows = layout.rows

    def body(t_ref, w_ref, out_ref, sem):
        place = Place()

        @pl.when(place.end)
        def _():
            start = place.far * layout.width + place.seat * layout.deep
            run_copies(
                [
                    pltpu.make_async_copy(
                        w_ref.at[pl.ds(pl.multiple_of(start + first, rows), rows)],
                        into,
                        sem.at[i],
                    )
                    for i, (first, into) in enumerate(layout.sides(out_ref))
                ]
            )

        @pl.when(jnp.logical_not(place.end))
        def _():
            run_copies(
                [pltpu.make_async_copy(t_ref.at[pl.ds(0, rows)], out_ref, sem.at[0])]
            )

    return call(
        held,
        body,
        array(rows, layout.width),
        [tokens, weight],
        [HBM, HBM],
        scratch=[pltpu.SemaphoreType.DMA((2,))],
        room=LARGE,
    )


def later_rows(held, tokens, layout):
    rows, cut = layout.rows, layout.cut

    def body(t_ref, out_ref, sem):
        start = pl.multiple_of(jnp.where(Place().end, 0, rows), rows)
        run_copies([pltpu.make_async_copy(t_ref.at[pl.ds(start, cut)], out_ref, sem)])

    return call(
        held,
        body,
        array(cut, layout.width),
        [tokens],
        [ANY],
        scratch=[pltpu.SemaphoreType.DMA],
    )


TALL = 32


def last_rows(held, tokens, across, coords, layout):
    cut, last = layout.sizes
    size = last + TALL
    wide = coords.shape[1]
    count = layout.tall // TALL

    def body(t_ref, a_ref, c_ref, out_ref, sem):
        place = Place()

        @pl.when(place.end)
        def _():
            copy = pltpu.make_async_copy(
                t_ref.at[pl.ds(cut, last)], out_ref.at[pl.ds(0, last)], sem
            )
            copy.start()
            for i in range(layout.width // wide):
                some = jnp.zeros((TALL, wide), out_ref.dtype)
                if i < count:
                    some = c_ref[i * TALL : (i + 1) * TALL, :].astype(out_ref.dtype)
                out_ref[last:, i * wide : (i + 1) * wide] = some
            copy.wait()

        @pl.when(jnp.logical_not(place.end))
        def _():
            run_copies([pltpu.make_async_copy(a_ref.at[pl.ds(0, size)], out_ref, sem)])

    return call(
        held,
        body,
        array(size, layout.width),
        [tokens, across, coords],
        [ANY, ANY, VMEM],
        scratch=[pltpu.SemaphoreType.DMA],
    )


def other_rows(held, across, layout):
    size = layout.sizes[1] + TALL
    rest = layout.tall - size

    def body(a_ref, out_ref, sem):
        run_copies([pltpu.make_async_copy(a_ref.at[pl.ds(size, rest)], out_ref, sem)])

    return call(
        held,
        body,
        array(rest, layout.width),
        [across],
        [ANY],
        scratch=[pltpu.SemaphoreType.DMA],
    )


def unpacked(held, coords, x, layout):
    last, wide = layout.sizes[1], coords.shape[1]

    def body(c_ref, x_ref, out_ref, rows_ref, below_ref, sem):
        copies = started(
            pltpu.make_async_copy(x_ref.at[pl.ds(last, TALL)], below_ref, sem.at[0]),
            pltpu.make_async_copy(x_ref.at[pl.ds(0, last)], rows_ref, sem.at[1]),
        )
        copies[0].wait()
        for i in range(layout.tall // TALL):
            some = pl.ds(i * TALL, TALL)
            other = below_ref[:, i * wide : (i + 1) * wide].astype(jnp.float32)
            out_ref[some, :] = (c_ref[some, :] + other).astype(out_ref.dtype)
        copies[1].wait()

    return call(
        held,
        body,
        [array(*coords.shape), array(last, layout.width)],
        [coords, x],
        [VMEM, ANY],
        scratch=[
            pltpu.VMEM((TALL, layout.width), jnp.bfloat16),
            pltpu.SemaphoreType.DMA((2,)),
        ],
    )


PARTS = 4


class Rows:
    def __init__(self, x_ref, start, held_ref, sem, begin=True):
        self.depth, self.held_ref, self.copies = held_ref.shape[0] // PARTS, held_ref, []
        for i in range(PARTS):
            some = pl.ds(pl.multiple_of(start + i * self.depth, 128), self.depth)
            self.copies.append(
                pltpu.make_async_copy(
                    x_ref.at[some], held_ref.at[pl.ds(i * self.depth, self.depth)], sem.at[i]
                )
            )
        if begin:
            started(*self.copies)

    def dot(self, a_ref):
        total = 0.0
        for i, copy in enumerate(self.copies):
            copy.wait()
            some = pl.ds(i * self.depth, self.depth)
            total += dot(a_ref[:, some], self.held_ref[some, :])
        return total


def started(*copies):
    for copy in copies:
        copy.start()
    return copies


def waited(copies):
    for copy in copies:
        copy.wait()


def room(count, layout):
    shape = (layout.width, layout.columns)
    return [
        x
        for _ in range(count)
        for x in (pltpu.VMEM(shape, jnp.bfloat16), pltpu.SemaphoreType.DMA((PARTS,)))
    ]


def sums(layout):
    return array(layout.tall, layout.columns, dtype=jnp.float32)


def sums_room(layout):
    return [
        pltpu.VMEM((layout.tall, layout.columns), jnp.float32),
        pltpu.SemaphoreType.DMA((10,)),
    ]


def own_block(held, tokens, weight, layout):
    def body(a_ref, w_ref, out_ref, held_ref, w_sem, a_held, sum_ref, sem):
        load = started(pltpu.make_async_copy(a_ref, a_held, sem.at[0]))
        w = Rows(w_ref, Place().own * layout.width, held_ref, w_sem)
        waited(load)
        sum_ref[...] = w.dot(a_held)
        run_copies([pltpu.make_async_copy(sum_ref, out_ref, sem.at[1])])

    return call(
        held,
        body,
        sums(layout),
        [tokens, weight],
        [ANY, HBM],
        [HBM],
        room(1, layout)
        + [pltpu.VMEM((layout.tall, layout.width), jnp.bfloat16)]
        + sums_room(layout),
        room=LARGE,
    )


def add_block(held, total, at_end, inside, weight, layout):
    width, tall = layout.width, layout.tall
    arrays = [*at_end[1], *inside[1]]

    def body(total_ref, w_ref, *refs):
        array_refs = list(refs[: len(arrays)])
        out_ref, w_held, w_sem, a_held, sum_ref, sem = refs[len(arrays) :]
        place = Place()

        def run(name, part_refs):
            w = Rows(w_ref, getattr(place, name) * width, w_held, w_sem)
            loads, start = [], 0
            for i, ref in enumerate(part_refs):
                into = a_held.at[pl.ds(start, ref.shape[0])]
                loads.append(pltpu.make_async_copy(ref, into, sem.at[i]))
                start += ref.shape[0]
            started(*loads)
            more = started(pltpu.make_async_copy(total_ref, sum_ref, sem.at[3]))
            waited(loads)
            some = w.dot(a_held)
            waited(more)
            sum_ref[...] += some
            run_copies([pltpu.make_async_copy(sum_ref, out_ref, sem.at[4])])

        for side, here in ((at_end, place.end), (inside, jnp.logical_not(place.end))):
            mine = [array_refs.pop(0) for _ in side[1]]
            pl.when(here)(lambda side=side, mine=mine: run(side[0], mine))

    return call(
        held,
        body,
        sums(layout),
        [total, weight, *arrays],
        [HBM, HBM] + [ANY] * len(arrays),
        [HBM],
        room(1, layout) + [pltpu.VMEM((tall, width), jnp.bfloat16)] + sums_room(layout),
        room=LARGE,
    )


def spread_of(use, low, place, count, adapters):
    some = [
        jnp.where(use == (place.mine ^ turn) * adapters + j, low, 0)
        for turn in range(count)
        for j in range(adapters)
    ]
    return jnp.concatenate(some, axis=1)


def terms_of(spread, ups_held):
    return dot(spread, ups_held).astype(jnp.bfloat16).astype(jnp.float32)


def add_last(held, total, low, use, ups, relayed, beyond, inner, weight, layout):
    adapters, rank, columns = ups[0].shape
    count = len(ups)
    cut, last = layout.sizes
    tall, width = layout.tall, layout.width

    def body(low_ref, use_ref, *refs):
        up_refs = refs[:count]
        total_ref, n0_ref, n1_ref, b0_ref, b1_ref, p0_ref, p1_ref, w_ref = refs[
            count : count + 8
        ]
        out_ref, sums_ref, *scratch = refs[count + 8 :]
        w_held, w_sem, v_held, v_sem, a_held, p_held, u_held, rows_ref, sum_ref, sem = scratch
        place = Place()
        first = n0_ref.shape[0]
        load = pltpu.make_async_copy(total_ref, sum_ref, sem.at[2])
        load.start()

        @pl.when(place.end)
        def _():
            w = Rows(w_ref, place.near * width, w_held, w_sem)
            loads = started(
                pltpu.make_async_copy(n0_ref, a_held.at[pl.ds(0, first)], sem.at[0]),
                pltpu.make_async_copy(n1_ref, a_held.at[pl.ds(first, tall - first)], sem.at[1]),
            )
            waited(loads)
            load.wait()
            sum_ref[...] += w.dot(a_held)
            run_copies([pltpu.make_async_copy(sum_ref, sums_ref, sem.at[7])])

        @pl.when(jnp.logical_not(place.end))
        def _():
            loads = started(
                *[
                    pltpu.make_async_copy(
                        up_ref,
                        u_held.at[pl.ds(i * adapters * rank, adapters * rank)],
                        sem.at[i + 3],
                    )
                    for i, up_ref in enumerate(up_refs)
                ]
            )
            beyonds = started(
                pltpu.make_async_copy(b0_ref, a_held.at[pl.ds(0, cut)], sem.at[0]),
                pltpu.make_async_copy(b1_ref, a_held.at[pl.ds(cut, last)], sem.at[1]),
            )
            w = Rows(w_ref, place.far * width, w_held, w_sem)
            inners = started(
                pltpu.make_async_copy(p0_ref, p_held.at[pl.ds(0, cut)], sem.at[8]),
                pltpu.make_async_copy(
                    p1_ref.at[pl.ds(0, last)], p_held.at[pl.ds(cut, last)], sem.at[9]
                ),
            )
            v = Rows(w_ref, place.partner * width, v_held, v_sem)
            spread = spread_of(use_ref[...], low_ref[...], place, count, adapters)
            waited(loads)
            terms = terms_of(spread, u_held[...])
            load.wait()
            sum_ref[...] += terms
            waited(beyonds)
            sum_ref[...] += w.dot(a_held)
            waited(inners)
            rows_ref[...] = (sum_ref[...] + v.dot(p_held)).astype(rows_ref.dtype)
            run_copies([pltpu.make_async_copy(rows_ref, out_ref, sem.at[7])])

    return call(
        held,
        body,
        [array(tall, columns), sums(layout)],
        [low, use, *[u.reshape(-1, columns) for u in ups]]
        + [total, *relayed, *beyond, *inner, weight],
        [VMEM] * 2 + [ANY] * count + [HBM] + [ANY] * 6 + [HBM],
        [ANY, HBM],
        room(2, layout)
        + [
            pltpu.VMEM((tall, width), jnp.bfloat16),
            pltpu.VMEM((tall, width), jnp.bfloat16),
            pltpu.VMEM((count * adapters * rank, columns), jnp.bfloat16),
            pltpu.VMEM((tall, columns), jnp.bfloat16),
        ]
        + sums_room(layout),
        room=LARGE,
    )


def helped(held, beyond, pieces, layout, i):
    size, width, columns = layout.sizes[i], layout.width, layout.columns
    count, deep = len(pieces), layout.deep

    def body(beyond_ref, *refs):
        piece_refs = refs[:count]
        out_ref, b_held, w_held, sem = refs[count:]
        place = Place()
        seat = place.seat

        @pl.when(jnp.logical_not(place.end))
        def _():
            load = started(pltpu.make_async_copy(beyond_ref, b_held, sem.at[0]))
            lends = started(
                *[
                    pltpu.make_async_copy(
                        part,
                        w_held.at[pl.ds(k * deep + first, layout.rows)],
                        sem.at[1 + 2 * k + side],
                    )
                    for k, piece_ref in enumerate(piece_refs)
                    for side, (first, part) in enumerate(layout.sides(piece_ref))
                ]
            )
            waited(load)
            total = 0.0
            step = count // 4
            for first in range(0, count, step):
                blocks = [
                    b_held[:, pl.ds(pl.multiple_of((seat ^ k) * deep, deep), deep)]
                    for k in range(first, first + step)
                ]
                waited(lends[2 * first : 2 * (first + step)])
                some = w_held[first * deep : (first + step) * deep, :]
                total += dot(jnp.concatenate(blocks, axis=1), some)
            out_ref[...] = total.astype(out_ref.dtype)

    return call(
        held,
        body,
        array(size, columns),
        [beyond, *pieces],
        [ANY] * (1 + count),
        scratch=[
            pltpu.VMEM((size, width), jnp.bfloat16),
            pltpu.VMEM((width, columns), jnp.bfloat16),
            pltpu.SemaphoreType.DMA((1 + 2 * count,)),
        ],
    )


NOT_KEPT = ("tick", "tokens", "down", "up", "use")


def first_finished(held, out, total, term, low, use, ups, layout):
    adapters, rank, columns = ups[0].shape
    count = len(ups)
    cut, last = layout.sizes

    def body(out_ref, total_ref, term_ref, low_ref, use_ref, *refs):
        up_refs = refs[:count]
        into_ref, late_ref, sum_ref, term_held, u_held, rows_ref, low_held, use_held, sem = refs[
            count:
        ]
        place = Place()

        @pl.when(place.end)
        def _():
            first = started(
                pltpu.make_async_copy(low_ref, low_held, sem.at[count + 2]),
                pltpu.make_async_copy(use_ref, use_held, sem.at[count + 3]),
            )
            loads = started(
                *[
                    pltpu.make_async_copy(
                        up_ref,
                        u_held.at[pl.ds(i * adapters * rank, adapters * rank)],
                        sem.at[i],
                    )
                    for i, up_ref in enumerate(up_refs)
                ],
                pltpu.make_async_copy(total_ref, sum_ref, sem.at[count]),
                pltpu.make_async_copy(term_ref, term_held, sem.at[count + 1]),
            )
            waited(first)
            spread = spread_of(use_held[...], low_held[...], place, count, adapters)
            waited(loads)
            sum_ref[...] += terms_of(spread, u_held[...])
            stores = started(
                pltpu.make_async_copy(sum_ref.at[pl.ds(cut, last)], late_ref, sem.at[0])
            )
            rows_ref[...] = (sum_ref[:cut, :] + term_held[...].astype(jnp.float32)).astype(
                rows_ref.dtype
            )
            run_copies([pltpu.make_async_copy(rows_ref, into_ref.at[pl.ds(0, cut)], sem.at[1])])
            waited(stores)

    return call(
        held,
        body,
        [array(layout.tall, columns), array(last, columns, dtype=jnp.float32)],
        [out, total, term, low, use, *[u.reshape(-1, columns) for u in ups]],
        [ANY, HBM] + [ANY] * (3 + count),
        [ANY, ANY],
        [
            pltpu.VMEM((layout.tall, columns), jnp.float32),
            pltpu.VMEM((cut, columns), jnp.bfloat16),
            pltpu.VMEM((count * adapters * rank, columns), jnp.bfloat16),
            pltpu.VMEM((cut, columns), jnp.bfloat16),
            pltpu.VMEM(low.shape, low.dtype),
            pltpu.VMEM(use.shape, use.dtype),
            pltpu.SemaphoreType.DMA((count + 4,)),
        ],
        alias={0: 0},
    )


def last_finished(held, out, late, term, layout):
    kept = [held[n] for n in sorted(held) if n.startswith("lent")]
    cut, last = layout.sizes

    def body(out_ref, late_ref, term_ref, *refs):
        into_ref, late_held, term_held, rows_ref, sem = refs[-5:]

        @pl.when(Place().end)
        def _():
            run_copies(
                [
                    pltpu.make_async_copy(late_ref, late_held, sem.at[0]),
                    pltpu.make_async_copy(term_ref, term_held, sem.at[1]),
                ]
            )
            rows_ref[...] = (late_held[...] + term_held[...].astype(jnp.float32)).astype(
                rows_ref.dtype
            )
            run_copies(
                [pltpu.make_async_copy(rows_ref, into_ref.at[pl.ds(cut, last)], sem.at[2])]
            )

    return call(
        held,
        body,
        array(*out.shape),
        [out, late, term, *kept],
        [ANY] * (3 + len(kept)),
        [ANY],
        [
            pltpu.VMEM((last, layout.columns), jnp.float32),
            pltpu.VMEM((last, layout.columns), out.dtype),
            pltpu.VMEM((last, layout.columns), out.dtype),
            pltpu.SemaphoreType.DMA((3,)),
        ],
        alias={0: 0},
    )


def coords_of(held, tokens, use, downs, turns, before=None):
    adapters, rank = downs[0].shape[0], downs[0].shape[1]
    count = len(downs)

    def body(use_ref, tokens_ref, *refs):
        out_ref, sent_ref = refs[-2:]
        mine = Place().mine
        total = refs[count][...] if before is not None else 0.0
        for turn, down_ref in zip(turns, refs[:count]):
            coords = lax.dot_general(
                tokens_ref[...],
                down_ref[...],
                (((1,), (1,)), ((), ())),
                preferred_element_type=jnp.float32,
            )
            for j in range(adapters):
                some = coords[:, j * rank : (j + 1) * rank]
                mask = use_ref[...] == (mine ^ turn) * adapters + j
                total = total + jnp.where(mask, some, 0.0)
        out_ref[...] = total
        sent_ref[...] = total.astype(sent_ref.dtype)

    flat = [d.reshape(-1, d.shape[2]) for d in downs]
    more = [] if before is None else [before]
    shape = (tokens.shape[0], rank)
    return call(
        held,
        body,
        [array(*shape, dtype=jnp.float32), array(*shape)],
        [use, tokens, *flat, *more],
        [VMEM] * (2 + count + len(more)),
    )


def added(held, a, b):
    def body(a_ref, b_ref, out_ref):
        sums = a_ref[...].astype(jnp.float32) + b_ref[...].astype(jnp.float32)
        out_ref[...] = sums.astype(out_ref.dtype)

    return call(held, body, array(*a.shape), [a, b], [VMEM] * 2)


def chained(tokens, tables, weight, down, up):
    layout = Layout(tokens, weight)
    across = hop_middle(tokens)
    h = dict(tick=jnp.zeros((8, 128), jnp.float32), down=down, up=up, tokens=tokens)
    h["ids"], h["slots"], h["blocks"] = tables
    h["first"] = first_rows(h, tokens, weight, layout)
    fence(h)
    first_p = hop(h["first"], PAIRS)
    fence(h)
    down_x = swap(h["down"], "pool")
    fence(h)
    down_c = swap(h["down"], "inner")
    fence(h)
    h["later"] = later_rows(h, h["tokens"], layout)
    h["down_c"] = down_c
    fence(h)
    later_p = hop(h["later"], PAIRS)
    fence(h)
    slot, rank = slot_and_rank(h.pop("ids"), h.pop("slots"), h.pop("blocks"))
    row = jnp.arange(MAXIMUM_RANK, dtype=jnp.int32)[None, :]
    h["use"] = jnp.where(row < rank[:, None], slot[:, None], -1)
    total = own_block(h, h["tokens"], weight, layout)
    h["lent"] = first_p
    fence(h)
    lent_y = swap_inside(h["lent"], "groups")
    fence(h)
    coords, _ = coords_of(h, h["tokens"], h["use"], [h["down"], h["down_c"]], [0, 1])
    h["down_x"] = down_x
    fence(h)
    lent_x = swap_inside(h["lent"], "pool")
    fence(h)
    down_xc = swap(h["down_x"], "inner")
    fence(h)
    coords, _ = coords_of(h, h["tokens"], h["use"], [h["down_x"]], [2], coords)
    h["down_xc"] = down_xc
    fence(h)
    coords, _ = coords_of(h, h["tokens"], h["use"], [h["down_xc"]], [3], coords)
    h["across"] = across
    fence(h)
    h["last"] = last_rows(h, h["tokens"], h["across"], coords, layout)
    h["later_p"], h["lent_y"] = later_p, lent_y
    fence(h)
    last_p = hop(h["last"], PAIRS)
    fence(h)
    beyond0 = hop_middle(h["later_p"])
    h["lent_x"] = lent_x
    fence(h)
    lent_d = swap_inside(h["lent_x"], "groups")
    fence(h)
    lent_c = swap_inside(h["lent"], "inner")
    fence(h)
    lent_yc = swap_inside(h["lent_y"], "inner")
    fence(h)
    h["others"] = other_rows(h, h["across"], layout)
    h["lent_c"], h["lent_yc"] = lent_c, lent_yc
    fence(h)
    others_o = hop(h["others"], OUTWARD)
    fence(h)
    lent_xc = swap_inside(h["lent_x"], "inner")
    fence(h)
    at_end = ("partner", [h["lent"], h["later_p"]])
    total = add_block(h, total, at_end, ("near", [h["across"]]), weight, layout)
    h["lent_xc"], h["lent_d"] = lent_xc, lent_d
    fence(h)
    lent_dc = swap_inside(h["lent_d"], "inner")
    h["lent_dc"], h["last_p"] = lent_dc, last_p
    fence(h)
    h["pair"], h["last_in"] = unpacked(h, coords, h["last_p"], layout)
    fence(h)
    pair_m = hop_middle(h["pair"])
    fence(h)
    beyond1 = hop_middle(h["last_in"])
    fence(h)
    up_x = swap(h["up"], "pool")
    h["beyond0"] = beyond0
    fence(h)
    names = ("lent", "lent_c", "lent_x", "lent_xc", "lent_y", "lent_yc", "lent_d", "lent_dc")
    pieces = [h[n] for n in names]
    h["help0"] = helped(h, h["beyond0"], pieces, layout, 0)
    h["pair_m"] = pair_m
    fence(h)
    help_o0 = hop(h["help0"], OUTWARD)
    fence(h)
    h["whole"] = added(h, h["pair"], h["pair_m"])
    fence(h)
    low_o = hop(h["whole"], OUTWARD)
    h["beyond1"], h["others_o"], h["up_x"] = beyond1, others_o, up_x
    fence(h)
    up_xc, up_c = swap(h["up_x"], "inner"), swap(h["up"], "inner")
    fence(h)
    pieces = [h[n] for n in names]
    h["help1"] = helped(h, h["beyond1"], pieces, layout, 1)
    h["up_xc"], h["up_c"] = up_xc, up_c
    fence(h)
    help_o1 = hop(h["help1"], OUTWARD)
    fence(h)
    ups = [h["up"], h["up_c"], h["up_x"], h["up_xc"]]
    out, total = add_last(
        h,
        total,
        h["whole"],
        h["use"],
        ups,
        [h["last_p"], h["others_o"]],
        [h["beyond0"], h["beyond1"]],
        [h["later_p"], h["last_p"]],
        weight,
        layout,
    )
    fence(h)
    h["help_o0"], h["low_o"] = help_o0, low_o
    fence(h)
    ups = [h["up"], h["up_c"], h["up_x"], h["up_xc"]]
    out, late = first_finished(h, out, total, h["help_o0"], h["low_o"], h["use"], ups, layout)
    fence(h)
    h["help_o1"] = help_o1
    fence(h)
    return last_finished(h, out, late, h.pop("help_o1"), layout)


def owner_mask(slot, rank, adapters):
    which = slot[:, None, None] == jnp.arange(adapters, dtype=jnp.int32)[None, :, None]
    within = jnp.arange(MAXIMUM_RANK, dtype=jnp.int32)[None, None, :] < rank[:, None, None]
    return jnp.logical_and(which, within)


def gathered(tokens, tables, weight, down, up):
    slot, rank = slot_and_rank(*tables)
    axes = ("pool", "inner")
    base = jnp.dot(
        lax.all_gather(tokens, "tensor", axis=1, tiled=True),
        weight,
        preferred_element_type=jnp.float32,
    )
    downs = lax.all_gather(down, axes, axis=0, tiled=True)
    ups = lax.all_gather(up, axes, axis=0, tiled=True)
    mask = owner_mask(slot, rank, downs.shape[0])
    coords = lax.dot_general(
        tokens,
        downs.reshape(-1, downs.shape[2]),
        (((1,), (1,)), ((), ())),
        preferred_element_type=jnp.float32,
    ).reshape(mask.shape)
    coords = jnp.sum(jnp.where(mask, coords, 0.0), axis=1)
    low_rank = lax.psum(coords, "tensor").astype(jnp.bfloat16)
    spread = jnp.where(mask, low_rank[:, None, :], jnp.zeros((), jnp.bfloat16))
    delta = jnp.dot(
        spread.reshape(spread.shape[0], -1),
        ups.reshape(-1, ups.shape[2]),
        preferred_element_type=jnp.float32,
    ).astype(jnp.bfloat16)
    return (base + delta.astype(jnp.float32)).astype(jnp.bfloat16)


def shards(
    tokens,
    token_adapter_ids,
    adapter_pool_slot,
    adapter_rank_blocks,
    query_weight,
    pool_down_factors,
    pool_up_factors,
):
    tables = (token_adapter_ids, adapter_pool_slot, adapter_rank_blocks)
    whole_chain = tuple(lax.axis_size(a) for a in AXES) == (2, 4, 2, 2)
    run = chained if whole_chain else gathered
    return run(tokens, tables, query_weight, pool_down_factors, pool_up_factors)


def solution(mesh):
    in_specs = (
        P(("groups", "pool", "inner"), "tensor"),
        P(("groups", "pool", "inner")),
        P("groups"),
        P("groups"),
        P(None, "tensor"),
        P(("groups", "pool", "inner"), None, "tensor"),
        P(("groups", "pool", "inner"), None, "tensor"),
    )
    out_specs = P(("groups", "pool", "inner"), "tensor")
    return jax.shard_map(shards, mesh=mesh, in_specs=in_specs, out_specs=out_specs, check_vma=False)
```

```python
import itertools

import jax
import jax.numpy as jnp
import numpy as np
from jax import lax
from jax.experimental import pallas as pl
from jax.experimental.pallas import tpu as pltpu
from jax.sharding import PartitionSpec as P

MAXIMUM_RANK = 128
RBLK = 16
AXES = ("groups", "tensor", "pool", "inner")

PAIRS = [(0, 1), (1, 0), (2, 3), (3, 2)]
OUTWARD = [(1, 0), (2, 3)]


def lookup(indices, table):
    count = table.shape[0]
    match = indices[..., None] == jnp.arange(count, dtype=jnp.int32)
    return jnp.sum(jnp.where(match, table, 0), axis=-1)


def slot_and_rank(ids, slots, blocks):
    return lookup(ids, slots), RBLK * lookup(ids, blocks)


def swap(x, axis):
    return lax.ppermute(x, axis, [(0, 1), (1, 0)])


def inside(x, step):
    shape = (2, 4, 2, 2)
    pairs = []
    for place in itertools.product(*map(range, shape)):
        groups, z, pool, inner = place
        to = step(*place) if z in (1, 2) else (groups, z, pool, 1 - inner)
        pairs.append(tuple(int(np.ravel_multi_index(p, shape)) for p in (place, to)))
    return lax.ppermute(x, AXES, pairs)


def hop_middle(x):
    return inside(x, lambda g, z, p, i: (g, 3 - z, p, i))


def swap_inside(x, axis):
    steps = {
        "groups": lambda g, z, p, i: (1 - g, z, p, i),
        "pool": lambda g, z, p, i: (g, z, 1 - p, i),
        "inner": lambda g, z, p, i: (g, z, p, 1 - i),
    }
    return inside(x, steps[axis])


def hop(x, pairs):
    return lax.ppermute(x, "tensor", pairs)


VMEM = pl.BlockSpec(memory_space=pltpu.VMEM)
ANY = pl.BlockSpec(memory_space=pl.ANY)
HBM = pl.BlockSpec(memory_space=pltpu.HBM)


def call(held, body, out_shapes, operands, in_specs, out_specs=None, scratch=(), room=16, alias=None):
    single = not isinstance(out_shapes, list)
    shapes = [out_shapes] if single else out_shapes
    out_specs = out_specs or [VMEM] * len(shapes)
    ins, outs = len(operands), len(shapes)
    tick = held["tick"]

    def counted(*refs):
        into = refs[ins + 1 + outs]
        into[...] = refs[ins][...] + 1.0
        body(*refs[:ins], *refs[ins + 1 : ins + 1 + outs], *refs[ins + 2 + outs :])

    *results, held["tick"] = pl.pallas_call(
        counted,
        out_shape=[*shapes, jax.ShapeDtypeStruct(tick.shape, tick.dtype)],
        in_specs=[*in_specs, VMEM],
        out_specs=[*out_specs, VMEM],
        scratch_shapes=list(scratch),
        input_output_aliases=alias or {},
        cost_estimate=pl.CostEstimate(flops=10**12, bytes_accessed=0, transcendentals=0),
        compiler_params=pltpu.CompilerParams(vmem_limit_bytes=room << 20),
    )(*operands, tick)
    return results[0] if single else results


def fence(held):
    call(held, lambda: None, [], [], [])
    names = sorted(held)
    held.update(zip(names, lax.optimization_barrier(tuple(held[n] for n in names))))


def array(*shape, dtype=jnp.bfloat16):
    return jax.ShapeDtypeStruct(shape, dtype)


def dot(a, b):
    return jnp.dot(a, b, preferred_element_type=jnp.float32)


class Place:
    def __init__(self):
        z = lax.axis_index("tensor")
        self.own, self.partner = z, z ^ 1
        self.end = jnp.logical_or(z == 0, z == 3)
        self.near = jnp.where(self.end, 3 - self.partner, 3 - z)
        self.far = jnp.where(self.end, 3 - z, 3 - self.partner)
        self.seat = lax.axis_index(("groups", "pool", "inner"))
        self.mine = lax.axis_index(("pool", "inner"))


class Layout:
    def __init__(self, tokens, weight):
        self.tall, self.width = tokens.shape
        self.columns = weight.shape[1]
        self.deep = self.width // 8
        self.rows = self.deep // 2
        self.cut = self.tall - self.rows
        self.sizes = [self.cut, self.tall - self.cut]

    def sides(self, ref):
        for side in range(2):
            columns = pl.ds(side * self.columns, self.columns)
            yield side * self.rows, ref.at[:, columns]


def run_copies(copies):
    for copy in copies:
        copy.start()
    for copy in copies:
        copy.wait()


LARGE = 50


def first_rows(held, tokens, weight, layout):
    rows = layout.rows

    def body(t_ref, w_ref, out_ref, sem):
        place = Place()

        @pl.when(place.end)
        def _():
            start = place.far * layout.width + place.seat * layout.deep
            run_copies(
                [
                    pltpu.make_async_copy(
                        w_ref.at[pl.ds(pl.multiple_of(start + first, rows), rows)],
                        into,
                        sem.at[i],
                    )
                    for i, (first, into) in enumerate(layout.sides(out_ref))
                ]
            )

        @pl.when(jnp.logical_not(place.end))
        def _():
            run_copies(
                [pltpu.make_async_copy(t_ref.at[pl.ds(0, rows)], out_ref, sem.at[0])]
            )

    return call(
        held,
        body,
        array(rows, layout.width),
        [tokens, weight],
        [HBM, HBM],
        scratch=[pltpu.SemaphoreType.DMA((2,))],
        room=LARGE,
    )


def later_rows(held, tokens, layout):
    rows, cut = layout.rows, layout.cut

    def body(t_ref, out_ref, sem):
        start = pl.multiple_of(jnp.where(Place().end, 0, rows), rows)
        run_copies([pltpu.make_async_copy(t_ref.at[pl.ds(start, cut)], out_ref, sem)])

    return call(
        held,
        body,
        array(cut, layout.width),
        [tokens],
        [ANY],
        scratch=[pltpu.SemaphoreType.DMA],
    )


TALL = 32


def last_rows(held, tokens, across, coords, layout):
    cut, last = layout.sizes
    size = last + TALL
    wide = coords.shape[1]
    count = layout.tall // TALL

    def body(t_ref, a_ref, c_ref, out_ref, sem):
        place = Place()

        @pl.when(place.end)
        def _():
            copy = pltpu.make_async_copy(
                t_ref.at[pl.ds(cut, last)], out_ref.at[pl.ds(0, last)], sem
            )
            copy.start()
            for i in range(layout.width // wide):
                some = jnp.zeros((TALL, wide), out_ref.dtype)
                if i < count:
                    some = c_ref[i * TALL : (i + 1) * TALL, :].astype(out_ref.dtype)
                out_ref[last:, i * wide : (i + 1) * wide] = some
            copy.wait()

        @pl.when(jnp.logical_not(place.end))
        def _():
            run_copies([pltpu.make_async_copy(a_ref.at[pl.ds(0, size)], out_ref, sem)])

    return call(
        held,
        body,
        array(size, layout.width),
        [tokens, across, coords],
        [ANY, ANY, VMEM],
        scratch=[pltpu.SemaphoreType.DMA],
    )


def other_rows(held, across, layout):
    size = layout.sizes[1] + TALL
    rest = layout.tall - size

    def body(a_ref, out_ref, sem):
        run_copies([pltpu.make_async_copy(a_ref.at[pl.ds(size, rest)], out_ref, sem)])

    return call(
        held,
        body,
        array(rest, layout.width),
        [across],
        [ANY],
        scratch=[pltpu.SemaphoreType.DMA],
    )


def unpacked(held, coords, x, layout):
    last, wide = layout.sizes[1], coords.shape[1]

    def body(c_ref, x_ref, out_ref, rows_ref, below_ref, sem):
        copies = started(
            pltpu.make_async_copy(x_ref.at[pl.ds(last, TALL)], below_ref, sem.at[0]),
            pltpu.make_async_copy(x_ref.at[pl.ds(0, last)], rows_ref, sem.at[1]),
        )
        copies[0].wait()
        for i in range(layout.tall // TALL):
            some = pl.ds(i * TALL, TALL)
            other = below_ref[:, i * wide : (i + 1) * wide].astype(jnp.float32)
            out_ref[some, :] = (c_ref[some, :] + other).astype(out_ref.dtype)
        copies[1].wait()

    return call(
        held,
        body,
        [array(*coords.shape), array(last, layout.width)],
        [coords, x],
        [VMEM, ANY],
        scratch=[
            pltpu.VMEM((TALL, layout.width), jnp.bfloat16),
            pltpu.SemaphoreType.DMA((2,)),
        ],
    )


PARTS = 4


class Rows:
    def __init__(self, x_ref, start, held_ref, sem, begin=True):
        self.depth, self.held_ref, self.copies = held_ref.shape[0] // PARTS, held_ref, []
        for i in range(PARTS):
            some = pl.ds(pl.multiple_of(start + i * self.depth, 128), self.depth)
            self.copies.append(
                pltpu.make_async_copy(
                    x_ref.at[some], held_ref.at[pl.ds(i * self.depth, self.depth)], sem.at[i]
                )
            )
        if begin:
            started(*self.copies)

    def dot(self, a_ref):
        total = 0.0
        for i, copy in enumerate(self.copies):
            copy.wait()
            some = pl.ds(i * self.depth, self.depth)
            total += dot(a_ref[:, some], self.held_ref[some, :])
        return total


def started(*copies):
    for copy in copies:
        copy.start()
    return copies


def waited(copies):
    for copy in copies:
        copy.wait()


def room(count, layout):
    shape = (layout.width, layout.columns)
    return [
        x
        for _ in range(count)
        for x in (pltpu.VMEM(shape, jnp.bfloat16), pltpu.SemaphoreType.DMA((PARTS,)))
    ]


def sums(layout):
    return array(layout.tall, layout.columns, dtype=jnp.float32)


def sums_room(layout):
    return [
        pltpu.VMEM((layout.tall, layout.columns), jnp.float32),
        pltpu.SemaphoreType.DMA((10,)),
    ]


def own_block(held, tokens, weight, layout):
    def body(a_ref, w_ref, out_ref, held_ref, w_sem, a_held, sum_ref, sem):
        load = started(pltpu.make_async_copy(a_ref, a_held, sem.at[0]))
        w = Rows(w_ref, Place().own * layout.width, held_ref, w_sem)
        waited(load)
        sum_ref[...] = w.dot(a_held)
        run_copies([pltpu.make_async_copy(sum_ref, out_ref, sem.at[1])])

    return call(
        held,
        body,
        sums(layout),
        [tokens, weight],
        [ANY, HBM],
        [HBM],
        room(1, layout)
        + [pltpu.VMEM((layout.tall, layout.width), jnp.bfloat16)]
        + sums_room(layout),
        room=LARGE,
    )


def add_block(held, total, at_end, inside, weight, layout):
    width, tall = layout.width, layout.tall
    arrays = [*at_end[1], *inside[1]]

    def body(total_ref, w_ref, *refs):
        array_refs = list(refs[: len(arrays)])
        out_ref, w_held, w_sem, a_held, sum_ref, sem = refs[len(arrays) :]
        place = Place()

        def run(name, part_refs):
            w = Rows(w_ref, getattr(place, name) * width, w_held, w_sem)
            loads, start = [], 0
            for i, ref in enumerate(part_refs):
                into = a_held.at[pl.ds(start, ref.shape[0])]
                loads.append(pltpu.make_async_copy(ref, into, sem.at[i]))
                start += ref.shape[0]
            started(*loads)
            more = started(pltpu.make_async_copy(total_ref, sum_ref, sem.at[3]))
            waited(loads)
            some = w.dot(a_held)
            waited(more)
            sum_ref[...] += some
            run_copies([pltpu.make_async_copy(sum_ref, out_ref, sem.at[4])])

        for side, here in ((at_end, place.end), (inside, jnp.logical_not(place.end))):
            mine = [array_refs.pop(0) for _ in side[1]]
            pl.when(here)(lambda side=side, mine=mine: run(side[0], mine))

    return call(
        held,
        body,
        sums(layout),
        [total, weight, *arrays],
        [HBM, HBM] + [ANY] * len(arrays),
        [HBM],
        room(1, layout) + [pltpu.VMEM((tall, width), jnp.bfloat16)] + sums_room(layout),
        room=LARGE,
    )


def spread_of(use, low, place, count, adapters):
    some = [
        jnp.where(use == (place.mine ^ turn) * adapters + j, low, 0)
        for turn in range(count)
        for j in range(adapters)
    ]
    return jnp.concatenate(some, axis=1)


def terms_of(spread, ups_held):
    return dot(spread, ups_held).astype(jnp.bfloat16).astype(jnp.float32)


def add_last(held, total, low, use, ups, relayed, beyond, inner, weight, layout):
    adapters, rank, columns = ups[0].shape
    count = len(ups)
    cut, last = layout.sizes
    tall, width = layout.tall, layout.width

    def body(low_ref, use_ref, *refs):
        up_refs = refs[:count]
        total_ref, n0_ref, n1_ref, b0_ref, b1_ref, p0_ref, p1_ref, w_ref = refs[
            count : count + 8
        ]
        out_ref, sums_ref, *scratch = refs[count + 8 :]
        w_held, w_sem, v_held, v_sem, a_held, p_held, u_held, rows_ref, sum_ref, sem = scratch
        place = Place()
        first = n0_ref.shape[0]
        load = pltpu.make_async_copy(total_ref, sum_ref, sem.at[2])
        load.start()

        @pl.when(place.end)
        def _():
            w = Rows(w_ref, place.near * width, w_held, w_sem)
            loads = started(
                pltpu.make_async_copy(n0_ref, a_held.at[pl.ds(0, first)], sem.at[0]),
                pltpu.make_async_copy(n1_ref, a_held.at[pl.ds(first, tall - first)], sem.at[1]),
            )
            waited(loads)
            load.wait()
            sum_ref[...] += w.dot(a_held)
            run_copies([pltpu.make_async_copy(sum_ref, sums_ref, sem.at[7])])

        @pl.when(jnp.logical_not(place.end))
        def _():
            loads = started(
                *[
                    pltpu.make_async_copy(
                        up_ref,
                        u_held.at[pl.ds(i * adapters * rank, adapters * rank)],
                        sem.at[i + 3],
                    )
                    for i, up_ref in enumerate(up_refs)
                ]
            )
            beyonds = started(
                pltpu.make_async_copy(b0_ref, a_held.at[pl.ds(0, cut)], sem.at[0]),
                pltpu.make_async_copy(b1_ref, a_held.at[pl.ds(cut, last)], sem.at[1]),
            )
            w = Rows(w_ref, place.far * width, w_held, w_sem)
            inners = started(
                pltpu.make_async_copy(p0_ref, p_held.at[pl.ds(0, cut)], sem.at[8]),
                pltpu.make_async_copy(
                    p1_ref.at[pl.ds(0, last)], p_held.at[pl.ds(cut, last)], sem.at[9]
                ),
            )
            v = Rows(w_ref, place.partner * width, v_held, v_sem)
            spread = spread_of(use_ref[...], low_ref[...], place, count, adapters)
            waited(loads)
            terms = terms_of(spread, u_held[...])
            load.wait()
            sum_ref[...] += terms
            waited(beyonds)
            sum_ref[...] += w.dot(a_held)
            waited(inners)
            rows_ref[...] = (sum_ref[...] + v.dot(p_held)).astype(rows_ref.dtype)
            run_copies([pltpu.make_async_copy(rows_ref, out_ref, sem.at[7])])

    return call(
        held,
        body,
        [array(tall, columns), sums(layout)],
        [low, use, *[u.reshape(-1, columns) for u in ups]]
        + [total, *relayed, *beyond, *inner, weight],
        [VMEM] * 2 + [ANY] * count + [HBM] + [ANY] * 6 + [HBM],
        [ANY, HBM],
        room(2, layout)
        + [
            pltpu.VMEM((tall, width), jnp.bfloat16),
            pltpu.VMEM((tall, width), jnp.bfloat16),
            pltpu.VMEM((count * adapters * rank, columns), jnp.bfloat16),
            pltpu.VMEM((tall, columns), jnp.bfloat16),
        ]
        + sums_room(layout),
        room=LARGE,
    )


def helped(held, beyond, pieces, layout, i):
    size, width, columns = layout.sizes[i], layout.width, layout.columns
    count, deep = len(pieces), layout.deep

    def body(beyond_ref, *refs):
        piece_refs = refs[:count]
        out_ref, b_held, w_held, sem = refs[count:]
        place = Place()
        seat = place.seat

        @pl.when(jnp.logical_not(place.end))
        def _():
            load = started(pltpu.make_async_copy(beyond_ref, b_held, sem.at[0]))
            lends = started(
                *[
                    pltpu.make_async_copy(
                        part,
                        w_held.at[pl.ds(k * deep + first, layout.rows)],
                        sem.at[1 + 2 * k + side],
                    )
                    for k, piece_ref in enumerate(piece_refs)
                    for side, (first, part) in enumerate(layout.sides(piece_ref))
                ]
            )
            waited(load)
            total = 0.0
            step = count // 4
            for first in range(0, count, step):
                blocks = [
                    b_held[:, pl.ds(pl.multiple_of((seat ^ k) * deep, deep), deep)]
                    for k in range(first, first + step)
                ]
                waited(lends[2 * first : 2 * (first + step)])
                some = w_held[first * deep : (first + step) * deep, :]
                total += dot(jnp.concatenate(blocks, axis=1), some)
            out_ref[...] = total.astype(out_ref.dtype)

    return call(
        held,
        body,
        array(size, columns),
        [beyond, *pieces],
        [ANY] * (1 + count),
        scratch=[
            pltpu.VMEM((size, width), jnp.bfloat16),
            pltpu.VMEM((width, columns), jnp.bfloat16),
            pltpu.SemaphoreType.DMA((1 + 2 * count,)),
        ],
    )


NOT_KEPT = ("tick", "tokens", "down", "up", "use")


def first_finished(held, out, total, term, low, use, ups, layout):
    adapters, rank, columns = ups[0].shape
    count = len(ups)
    cut, last = layout.sizes

    def body(out_ref, total_ref, term_ref, low_ref, use_ref, *refs):
        up_refs = refs[:count]
        into_ref, late_ref, sum_ref, term_held, u_held, rows_ref, low_held, use_held, sem = refs[
            count:
        ]
        place = Place()

        @pl.when(place.end)
        def _():
            first = started(
                pltpu.make_async_copy(low_ref, low_held, sem.at[count + 2]),
                pltpu.make_async_copy(use_ref, use_held, sem.at[count + 3]),
            )
            loads = started(
                *[
                    pltpu.make_async_copy(
                        up_ref,
                        u_held.at[pl.ds(i * adapters * rank, adapters * rank)],
                        sem.at[i],
                    )
                    for i, up_ref in enumerate(up_refs)
                ],
                pltpu.make_async_copy(total_ref, sum_ref, sem.at[count]),
                pltpu.make_async_copy(term_ref, term_held, sem.at[count + 1]),
            )
            waited(first)
            spread = spread_of(use_held[...], low_held[...], place, count, adapters)
            waited(loads)
            sum_ref[...] += terms_of(spread, u_held[...])
            stores = started(
                pltpu.make_async_copy(sum_ref.at[pl.ds(cut, last)], late_ref, sem.at[0])
            )
            rows_ref[...] = (sum_ref[:cut, :] + term_held[...].astype(jnp.float32)).astype(
                rows_ref.dtype
            )
            run_copies([pltpu.make_async_copy(rows_ref, into_ref.at[pl.ds(0, cut)], sem.at[1])])
            waited(stores)

    return call(
        held,
        body,
        [array(layout.tall, columns), array(last, columns, dtype=jnp.float32)],
        [out, total, term, low, use, *[u.reshape(-1, columns) for u in ups]],
        [ANY, HBM] + [ANY] * (3 + count),
        [ANY, ANY],
        [
            pltpu.VMEM((layout.tall, columns), jnp.float32),
            pltpu.VMEM((cut, columns), jnp.bfloat16),
            pltpu.VMEM((count * adapters * rank, columns), jnp.bfloat16),
            pltpu.VMEM((cut, columns), jnp.bfloat16),
            pltpu.VMEM(low.shape, low.dtype),
            pltpu.VMEM(use.shape, use.dtype),
            pltpu.SemaphoreType.DMA((count + 4,)),
        ],
        alias={0: 0},
    )


def last_finished(held, out, late, term, layout):
    kept = []
    cut, last = layout.sizes

    def body(out_ref, late_ref, term_ref, *refs):
        into_ref, late_held, term_held, rows_ref, sem = refs[-5:]

        @pl.when(Place().end)
        def _():
            run_copies(
                [
                    pltpu.make_async_copy(late_ref, late_held, sem.at[0]),
                    pltpu.make_async_copy(term_ref, term_held, sem.at[1]),
                ]
            )
            rows_ref[...] = (late_held[...] + term_held[...].astype(jnp.float32)).astype(
                rows_ref.dtype
            )
            run_copies(
                [pltpu.make_async_copy(rows_ref, into_ref.at[pl.ds(cut, last)], sem.at[2])]
            )

    return call(
        held,
        body,
        array(*out.shape),
        [out, late, term, *kept],
        [ANY] * (3 + len(kept)),
        [ANY],
        [
            pltpu.VMEM((last, layout.columns), jnp.float32),
            pltpu.VMEM((last, layout.columns), out.dtype),
            pltpu.VMEM((last, layout.columns), out.dtype),
            pltpu.SemaphoreType.DMA((3,)),
        ],
        alias={0: 0},
    )


def coords_of(held, tokens, use, downs, turns, before=None):
    adapters, rank = downs[0].shape[0], downs[0].shape[1]
    count = len(downs)

    def body(use_ref, tokens_ref, *refs):
        out_ref, sent_ref = refs[-2:]
        mine = Place().mine
        total = refs[count][...] if before is not None else 0.0
        for turn, down_ref in zip(turns, refs[:count]):
            coords = lax.dot_general(
                tokens_ref[...],
                down_ref[...],
                (((1,), (1,)), ((), ())),
                preferred_element_type=jnp.float32,
            )
            for j in range(adapters):
                some = coords[:, j * rank : (j + 1) * rank]
                mask = use_ref[...] == (mine ^ turn) * adapters + j
                total = total + jnp.where(mask, some, 0.0)
        out_ref[...] = total
        sent_ref[...] = total.astype(sent_ref.dtype)

    flat = [d.reshape(-1, d.shape[2]) for d in downs]
    more = [] if before is None else [before]
    shape = (tokens.shape[0], rank)
    return call(
        held,
        body,
        [array(*shape, dtype=jnp.float32), array(*shape)],
        [use, tokens, *flat, *more],
        [VMEM] * (2 + count + len(more)),
    )


def added(held, a, b):
    def body(a_ref, b_ref, out_ref):
        sums = a_ref[...].astype(jnp.float32) + b_ref[...].astype(jnp.float32)
        out_ref[...] = sums.astype(out_ref.dtype)

    return call(held, body, array(*a.shape), [a, b], [VMEM] * 2)


def chained(tokens, tables, weight, down, up):
    layout = Layout(tokens, weight)
    across = hop_middle(tokens)
    h = dict(tick=jnp.zeros((8, 128), jnp.float32), down=down, up=up, tokens=tokens)
    h["ids"], h["slots"], h["blocks"] = tables
    h["first"] = first_rows(h, tokens, weight, layout)
    fence(h)
    first_p = hop(h["first"], PAIRS)
    fence(h)
    down_x = swap(h["down"], "pool")
    fence(h)
    down_c = swap(h["down"], "inner")
    fence(h)
    h["later"] = later_rows(h, h["tokens"], layout)
    h["down_c"] = down_c
    fence(h)
    later_p = hop(h["later"], PAIRS)
    fence(h)
    slot, rank = slot_and_rank(h.pop("ids"), h.pop("slots"), h.pop("blocks"))
    row = jnp.arange(MAXIMUM_RANK, dtype=jnp.int32)[None, :]
    h["use"] = jnp.where(row < rank[:, None], slot[:, None], -1)
    total = own_block(h, h["tokens"], weight, layout)
    h["lent"] = first_p
    fence(h)
    lent_y = swap_inside(h["lent"], "groups")
    fence(h)
    coords, _ = coords_of(h, h["tokens"], h["use"], [h["down"], h["down_c"]], [0, 1])
    h["down_x"] = down_x
    fence(h)
    lent_x = swap_inside(h["lent"], "pool")
    fence(h)
    down_xc = swap(h["down_x"], "inner")
    fence(h)
    coords, _ = coords_of(h, h["tokens"], h["use"], [h["down_x"]], [2], coords)
    h["down_xc"] = down_xc
    fence(h)
    coords, _ = coords_of(h, h["tokens"], h["use"], [h["down_xc"]], [3], coords)
    h["across"] = across
    fence(h)
    h["last"] = last_rows(h, h["tokens"], h["across"], coords, layout)
    h["later_p"], h["lent_y"] = later_p, lent_y
    fence(h)
    last_p = hop(h["last"], PAIRS)
    fence(h)
    beyond0 = hop_middle(h["later_p"])
    h["lent_x"] = lent_x
    fence(h)
    lent_d = swap_inside(h["lent_x"], "groups")
    fence(h)
    lent_c = swap_inside(h["lent"], "inner")
    fence(h)
    lent_yc = swap_inside(h["lent_y"], "inner")
    fence(h)
    h["others"] = other_rows(h, h["across"], layout)
    h["lent_c"], h["lent_yc"] = lent_c, lent_yc
    fence(h)
    others_o = hop(h["others"], OUTWARD)
    fence(h)
    lent_xc = swap_inside(h["lent_x"], "inner")
    fence(h)
    at_end = ("partner", [h["lent"], h["later_p"]])
    total = add_block(h, total, at_end, ("near", [h["across"]]), weight, layout)
    h["lent_xc"], h["lent_d"] = lent_xc, lent_d
    fence(h)
    lent_dc = swap_inside(h["lent_d"], "inner")
    h["lent_dc"], h["last_p"] = lent_dc, last_p
    fence(h)
    h["pair"], h["last_in"] = unpacked(h, coords, h["last_p"], layout)
    fence(h)
    pair_m = hop_middle(h["pair"])
    fence(h)
    beyond1 = hop_middle(h["last_in"])
    fence(h)
    up_x = swap(h["up"], "pool")
    h["beyond0"] = beyond0
    fence(h)
    names = ("lent", "lent_c", "lent_x", "lent_xc", "lent_y", "lent_yc", "lent_d", "lent_dc")
    pieces = [h[n] for n in names]
    h["help0"] = helped(h, h["beyond0"], pieces, layout, 0)
    h["pair_m"] = pair_m
    fence(h)
    help_o0 = hop(h["help0"], OUTWARD)
    fence(h)
    h["whole"] = added(h, h["pair"], h["pair_m"])
    fence(h)
    low_o = hop(h["whole"], OUTWARD)
    h["beyond1"], h["others_o"], h["up_x"] = beyond1, others_o, up_x
    fence(h)
    up_xc, up_c = swap(h["up_x"], "inner"), swap(h["up"], "inner")
    fence(h)
    pieces = [h[n] for n in names]
    h["help1"] = helped(h, h["beyond1"], pieces, layout, 1)
    h["up_xc"], h["up_c"] = up_xc, up_c
    fence(h)
    help_o1 = hop(h["help1"], OUTWARD)
    fence(h)
    ups = [h["up"], h["up_c"], h["up_x"], h["up_xc"]]
    out, total = add_last(
        h,
        total,
        h["whole"],
        h["use"],
        ups,
        [h["last_p"], h["others_o"]],
        [h["beyond0"], h["beyond1"]],
        [h["later_p"], h["last_p"]],
        weight,
        layout,
    )
    fence(h)
    h["help_o0"], h["low_o"] = help_o0, low_o
    fence(h)
    ups = [h["up"], h["up_c"], h["up_x"], h["up_xc"]]
    out, late = first_finished(h, out, total, h["help_o0"], h["low_o"], h["use"], ups, layout)
    fence(h)
    h["help_o1"] = help_o1
    fence(h)
    return last_finished(h, out, late, h.pop("help_o1"), layout)


def owner_mask(slot, rank, adapters):
    which = slot[:, None, None] == jnp.arange(adapters, dtype=jnp.int32)[None, :, None]
    within = jnp.arange(MAXIMUM_RANK, dtype=jnp.int32)[None, None, :] < rank[:, None, None]
    return jnp.logical_and(which, within)


def gathered(tokens, tables, weight, down, up):
    slot, rank = slot_and_rank(*tables)
    axes = ("pool", "inner")
    base = jnp.dot(
        lax.all_gather(tokens, "tensor", axis=1, tiled=True),
        weight,
        preferred_element_type=jnp.float32,
    )
    downs = lax.all_gather(down, axes, axis=0, tiled=True)
    ups = lax.all_gather(up, axes, axis=0, tiled=True)
    mask = owner_mask(slot, rank, downs.shape[0])
    coords = lax.dot_general(
        tokens,
        downs.reshape(-1, downs.shape[2]),
        (((1,), (1,)), ((), ())),
        preferred_element_type=jnp.float32,
    ).reshape(mask.shape)
    coords = jnp.sum(jnp.where(mask, coords, 0.0), axis=1)
    low_rank = lax.psum(coords, "tensor").astype(jnp.bfloat16)
    spread = jnp.where(mask, low_rank[:, None, :], jnp.zeros((), jnp.bfloat16))
    delta = jnp.dot(
        spread.reshape(spread.shape[0], -1),
        ups.reshape(-1, ups.shape[2]),
        preferred_element_type=jnp.float32,
    ).astype(jnp.bfloat16)
    return (base + delta.astype(jnp.float32)).astype(jnp.bfloat16)


def shards(
    tokens,
    token_adapter_ids,
    adapter_pool_slot,
    adapter_rank_blocks,
    query_weight,
    pool_down_factors,
    pool_up_factors,
):
    tables = (token_adapter_ids, adapter_pool_slot, adapter_rank_blocks)
    whole_chain = tuple(lax.axis_size(a) for a in AXES) == (2, 4, 2, 2)
    run = chained if whole_chain else gathered
    return run(tokens, tables, query_weight, pool_down_factors, pool_up_factors)


def solution(mesh):
    in_specs = (
        P(("groups", "pool", "inner"), "tensor"),
        P(("groups", "pool", "inner")),
        P("groups"),
        P("groups"),
        P(None, "tensor"),
        P(("groups", "pool", "inner"), None, "tensor"),
        P(("groups", "pool", "inner"), None, "tensor"),
    )
    out_specs = P(("groups", "pool", "inner"), "tensor")
    return jax.shard_map(shards, mesh=mesh, in_specs=in_specs, out_specs=out_specs, check_vma=False)
```
